32 devices in a mesh: batch: 16 (over z, y, core), seq: 2 (over x).
Axes of the slice: x: 2, y: 2, z: 4, core: 2. Of those that a mesh axis runs over, the one named last changes fastest.
Arguments:
- block_in: bfloat16 [16, 1024, 1024], P('batch', 'seq'), may hold values from -2.5 to 2.5
- conditioning: bfloat16 [16, 1024], P('batch'), may hold values from -2.5 to 2.5
- cotangent: bfloat16 [16, 1024, 1024], P('batch', 'seq'), may hold values from -2.5 to 2.5
- ada_weight: bfloat16 [1024, 6144], P(('batch', 'seq')), may hold values from -0.25 to 0.25
- ada_bias: bfloat16 [6144], P(('batch', 'seq')), may hold values from -1.25 to 1.25
- qkv_weight: bfloat16 [1024, 3072], P(('batch', 'seq')), may hold values from -0.1875 to 0.1875
- qv_bias: bfloat16 [2048], P(('batch', 'seq')), may hold values from -1.25 to 1.25
- out_weight: bfloat16 [1024, 1024], P(('batch', 'seq')), may hold values from -1.5 to 1.5
- out_bias: bfloat16 [1024], P(('batch', 'seq')), may hold values from -1.25 to 1.25
- up_weight: bfloat16 [1024, 4096], P(('batch', 'seq')), may hold values from -0.1875 to 0.1875
- up_bias: bfloat16 [4096], P(('batch', 'seq')), may hold values from -1.25 to 1.25
- down_weight: bfloat16 [4096, 1024], P(('batch', 'seq')), may hold values from -0.09375 to 0.09375
- down_bias: bfloat16 [1024], P(('batch', 'seq')), may hold values from -1.25 to 1.25
Outputs:
- block_out: bfloat16 [16, 1024, 1024], P('batch', 'seq')
- input_grad: bfloat16 [16, 1024, 1024], P('batch', 'seq')
- cond_grad: bfloat16 [16, 1024], P('batch')
- ada_weight_grad: float32 [1024, 6144], P(('batch', 'seq'))
- ada_bias_grad: float32 [6144], P(('batch', 'seq'))
- qkv_weight_grad: float32 [1024, 3072], P(('batch', 'seq'))
- qv_bias_grad: float32 [2048], P(('batch', 'seq'))
- out_weight_grad: float32 [1024, 1024], P(('batch', 'seq'))
- out_bias_grad: float32 [1024], P(('batch', 'seq'))
- up_weight_grad: float32 [1024, 4096], P(('batch', 'seq'))
- up_bias_grad: float32 [4096], P(('batch', 'seq'))
- down_weight_grad: float32 [4096, 1024], P(('batch', 'seq'))
- down_bias_grad: float32 [1024], P(('batch', 'seq'))
The draws below stay inside these ranges and needn't reach their ends.
All inputs are finite; a program needn't handle non-finite values.
Results may differ from the reference program's by a relative error of at most 0.015.
The reference program's roundings to bfloat16 on the way count: a program that leaves them out, or rounds other values in their place, can miss the bound.
Values may be sent and summed in bfloat16 or wider, within the bound.
No kernel may reach another device: no remote copies, remote signals or barrier semaphores. Data moves between devices by JAX's collectives and lax.ppermute only.
A program may use at most 256 MiB of HBM per device.

```python
import jax
import jax.numpy as jnp
from jax import lax

D = 1024
HEADS = 16
HEAD_DIM = 64
FF = 4096
LEN = 1024
LATENTS = 16


def level_of(own_key, extent, cuts, low, high):
    level, own = 1.0, jax.random.fold_in(own_key, 6)
    for axis_at, shards_of in cuts:
        heights = jnp.exp(jax.random.uniform(jax.random.fold_in(own, axis_at), (shards_of,), jnp.float32, low / len(cuts), high / len(cuts)))
        level = level * jnp.repeat(heights, extent[axis_at] // shards_of).reshape([-1 if axis == axis_at else 1 for axis in range(len(extent))])
    return level


def bell_draw(own_key, dims, scale, bound, shards=(), held_as=jnp.bfloat16):
    drawn = jax.random.normal(own_key, dims, jnp.float32) * scale
    if len(shards) > 0:
        drawn = level_of(own_key, dims, shards, -0.22, 0.18) * drawn
    return jnp.clip(drawn, min=-bound, max=bound).astype(held_as)


def setup_inputs(seed: int = 0) -> dict:
    key_list = jax.random.split(jax.random.key(seed), 14)
    return {
        "block_in": bell_draw(key_list[0], (LATENTS, LEN, D), 1.0, 2.5, ((0, 16), (1, 2))),
        "conditioning": bell_draw(key_list[1], (LATENTS, D), 1.0, 2.5, ((0, 16),)),
        "cotangent": bell_draw(key_list[2], (LATENTS, LEN, D), 1.0, 2.5, ((0, 16), (1, 2))),
        "ada_weight": bell_draw(key_list[3], (D, 6 * D), (D // 2) ** -0.5, 0.25, ((0, 32),)),
        "ada_bias": bell_draw(key_list[4], (6 * D,), 0.5, 1.25, ((0, 32),)),
        "qkv_weight": bell_draw(key_list[5], (D, 3 * D), D ** -0.5, 0.1875, ((0, 32),)),
        "qv_bias": bell_draw(key_list[6], (2 * D,), 0.5, 1.25, ((0, 32),)),
        "out_weight": bell_draw(key_list[7], (D, D), (D // 64) ** -0.5, 1.5, ((0, 32),)),
        "out_bias": bell_draw(key_list[8], (D,), 0.5, 1.25, ((0, 32),)),
        "up_weight": bell_draw(key_list[9], (D, FF), D ** -0.5, 0.1875, ((0, 32),)),
        "up_bias": bell_draw(key_list[10], (FF,), 0.5, 1.25, ((0, 32),)),
        "down_weight": bell_draw(key_list[11], (FF, D), FF ** -0.5, 0.09375, ((0, 32),)),
        "down_bias": bell_draw(key_list[12], (D,), 0.5, 1.25, ((0, 32),)),
    }


@jax.custom_vjp
def low(v):
    return lax.optimization_barrier(v.astype(jnp.bfloat16)).astype(jnp.float32)

@jax.custom_vjp
def low_back(v):
    return v

def low_keep(v):
    return (low(v), None)

def low_pass(kept, grad):
    return (grad,)

def back_keep(v):
    return (v, None)

def back_low(kept, grad):
    return (low(grad),)
low.defvjp(low_keep, low_pass)
low_back.defvjp(back_keep, back_low)
HIGHEST = lax.Precision.HIGHEST
EPSILON = 1e-06

def modulate(values, shifts, scales):
    average = lax.optimization_barrier(jnp.mean(values, axis=-1, keepdims=True))
    centered = values - average
    variance = lax.optimization_barrier(jnp.mean(centered * centered, axis=-1, keepdims=True))
    return centered * lax.rsqrt(variance + EPSILON) * (1.0 + scales) + shifts

def latent_forward(latent_in, cond_vec, ada_weight, ada_bias, qkv_weight, qv_bias, out_weight, out_bias, up_weight, up_bias, down_weight, down_bias):
    cond_act = low(jax.nn.silu(cond_vec))
    modulation = jnp.dot(cond_act, ada_weight, precision=HIGHEST) + ada_bias
    shift_attn, scale_attn, gate_attn, shift_mlp, scale_mlp, gate_mlp = jnp.split(modulation, 6)
    modded_attn = low(modulate(latent_in, shift_attn, scale_attn))
    qkv_bias = jnp.concatenate([qv_bias[:D], jnp.zeros((D,), jnp.float32), qv_bias[D:]])
    qkv_proj = low(low_back(jnp.dot(modded_attn, qkv_weight, precision=HIGHEST) + qkv_bias))
    queries = qkv_proj[:, :D].reshape(LEN, HEADS, HEAD_DIM)
    key_part = qkv_proj[:, D:2 * D].reshape(LEN, HEADS, HEAD_DIM)
    value_part = qkv_proj[:, 2 * D:].reshape(LEN, HEADS, HEAD_DIM)
    scores = low_back(jnp.einsum('qhd,khd->hqk', queries, key_part, precision=HIGHEST) * HEAD_DIM ** (-0.5))
    probs = low(jax.nn.softmax(scores, axis=-1))
    attended = jnp.einsum('hqk,khd->qhd', probs, value_part, precision=HIGHEST).reshape(LEN, D)
    attended = low(low_back(attended))
    attn_proj = low_back(jnp.dot(attended, out_weight, precision=HIGHEST) + out_bias)
    middle = latent_in + gate_attn * attn_proj
    modded_mlp = low(modulate(middle, shift_mlp, scale_mlp))
    pre_act = low_back(jnp.dot(modded_mlp, up_weight, precision=HIGHEST) + up_bias)
    activated = low(jax.nn.gelu(pre_act, approximate=True))
    mlp_proj = low_back(jnp.dot(activated, down_weight, precision=HIGHEST) + down_bias)
    return middle + gate_mlp * mlp_proj

def reference(block_in, conditioning, cotangent, ada_weight, ada_bias, qkv_weight, qv_bias, out_weight, out_bias, up_weight, up_bias, down_weight, down_bias):
    weights = tuple((weight.astype(jnp.float32) for weight in (ada_weight, ada_bias, qkv_weight, qv_bias, out_weight, out_bias, up_weight, up_bias, down_weight, down_bias)))

    def one_latent(totals, items):
        latent_in, cond_vec, latent_cot = items
        output, pullback = jax.vjp(latent_forward, latent_in.astype(jnp.float32), cond_vec.astype(jnp.float32), *weights)
        grads = pullback(latent_cot.astype(jnp.float32))
        totals = tuple((left + right for left, right in zip(totals, grads[2:])))
        return (totals, (output.astype(jnp.bfloat16), grads[0].astype(jnp.bfloat16), grads[1].astype(jnp.bfloat16)))
    zeros = tuple((jnp.zeros(weight.shape, jnp.float32) for weight in weights))
    totals, outputs = lax.scan(one_latent, zeros, (block_in, conditioning, cotangent))
    return (outputs[0], outputs[1], outputs[2], totals[0], totals[1], totals[2], totals[3], totals[4], totals[5], totals[6], totals[7], totals[8], totals[9])
```

```python
from functools import partial

import jax
import jax.numpy as jnp
import numpy as np
from jax import lax
from jax.experimental import pallas as pl
from jax.experimental.pallas import tpu as pltpu
from jax.sharding import PartitionSpec as P

HEAD_DIM = 64
SCALE = HEAD_DIM**-0.5
EPSILON = 1e-06
HIGHEST = lax.Precision.HIGHEST
F32, BF16 = jnp.float32, jnp.bfloat16
AXES = ("batch", "seq")
VMEM_LIMIT = 56 * 1024 * 1024
TILE = 256


def dot(left, right, dims, kind=F32):
    out = lax.dot_general(left, right, ((dims[:1], dims[1:]), ((), ())), preferred_element_type=F32)
    return out.astype(kind)


def modulate(values, shifts, scales):
    average = jnp.mean(values, axis=-1, keepdims=True)
    centered = values - average
    variance = jnp.mean(centered * centered, axis=-1, keepdims=True)
    return centered * lax.rsqrt(variance + EPSILON) * (1.0 + scales) + shifts


class Grid:
    def __init__(self, mesh):
        batch, seq = mesh.shape["batch"], mesh.shape["seq"]
        self.size = {"z": batch // 4, "y": 2, "c": 2, "s": seq}
        self.shape = tuple(self.size.values())
        self.count = batch * seq

    def locate(self):
        batch, seq = lax.axis_index("batch"), lax.axis_index("seq")
        self.at = {"z": batch // 4, "y": (batch // 2) % 2, "c": batch % 2, "s": seq}
        self.me = batch * self.size["s"] + seq

    def send(self, value, **steps):
        moves = [steps.get(name, 0) for name in self.size]
        pairs = []
        for place in np.ndindex(*self.shape):
            target = tuple((p + m) % n for p, m, n in zip(place, moves, self.shape))
            pairs.append(
                (int(np.ravel_multi_index(place, self.shape)), int(np.ravel_multi_index(target, self.shape)))
            )
        return lax.ppermute(value, AXES, pairs)

    def arrivals(self, value, name):
        return [value] + [self.send(value, **{name: d}) for d in range(1, self.size[name])]

    def gather(self, value, name):
        return jnp.concatenate([part[None] for part in self.arrivals(value, name)])

    def gather_rows(self, value, order):
        for name in order[:-1]:
            value = jnp.concatenate([part[None] for part in self.arrivals(value, name)])
        parts = self.arrivals(value, order[-1])
        names = tuple(reversed(order))
        steps = [dict(zip(names, at)) for at in np.ndindex(*[self.size[name] for name in names])]
        lead = len(order) - 1
        return [part.reshape((-1,) + part.shape[lead:]) for part in parts], steps

    def reduce(self, terms, axis, name, kind):
        n, me = self.size[name], self.at[name]
        total = lax.dynamic_index_in_dim(terms, me, axis, keepdims=False).astype(F32)
        for d in range(1, n):
            part = lax.dynamic_index_in_dim(terms, (me + d) % n, axis, keepdims=False)
            total = total + self.send(part, **{name: d}).astype(F32)
        return total.astype(kind)

    def shard_of(self, back):
        index = 0
        for name, n in self.size.items():
            index = index * n + (self.at[name] - back.get(name, 0)) % n
        return index

    def to_latents(self, terms):
        for axis, name in ((2, "c"), (1, "y"), (0, "z")):
            terms = self.reduce(terms, axis, name, F32)
        return sum(self.arrivals(terms, "s"))


def place_kernel(jobs, flat, table, *refs):
    pieces, out, sems = refs[:-2], refs[-2], refs[-1]
    copies = []
    for at, (piece, block, unit, part) in enumerate(jobs):
        source = pieces[piece].at[block, unit]
        rows, columns = source.shape
        if flat:
            target = out.at[
                pl.ds(pl.multiple_of(table[at] * rows, rows), rows), pl.ds(part * columns, columns)
            ]
        else:
            target = out.at[table[at], part]
        copies.append(pltpu.make_async_copy(source, target, sems.at[at]))
        copies[-1].start()
    for copy in copies:
        copy.wait()


def place(pieces, jobs, table):
    rows, columns = pieces[0].shape[2:]
    parts = 1 + max(job[3] for job in jobs)
    count = len(jobs) // parts
    flat = rows % 16 == 0
    out = pl.pallas_call(
        partial(place_kernel, jobs, flat),
        out_shape=jax.ShapeDtypeStruct(
            (count * rows, parts * columns) if flat else (count, parts, rows, columns), pieces[0].dtype
        ),
        grid_spec=pltpu.PrefetchScalarGridSpec(
            num_scalar_prefetch=1,
            in_specs=[pl.BlockSpec(memory_space=pl.ANY)] * len(pieces),
            out_specs=pl.BlockSpec(memory_space=pltpu.VMEM if flat else pl.ANY),
            scratch_shapes=[pltpu.SemaphoreType.DMA((len(jobs),))],
        ),
        compiler_params=pltpu.CompilerParams(vmem_limit_bytes=VMEM_LIMIT),
        cost_estimate=pl.CostEstimate(
            flops=0, bytes_accessed=4 * len(jobs) * rows * columns, transcendentals=0
        ),
    )(jnp.stack(table).astype(jnp.int32), *pieces)
    if not flat:
        out = out.transpose(0, 2, 1, 3).reshape(count * rows, parts * columns)
    return out


def head_mask(width, head):
    lanes = lax.broadcasted_iota(jnp.int32, (1, width), 1)
    return (lanes >= head * HEAD_DIM) & (lanes < (head + 1) * HEAD_DIM)


def attend_kernel(width, qkv, out, logsum):
    tokens = qkv.shape[1]
    step = min(128, width)
    tile = min(TILE, tokens)
    for start in range(0, width, step):
        keys = qkv[0, :, width + start : width + start + step]
        values = qkv[0, :, 2 * width + start : 2 * width + start + step]
        for row in range(0, tokens, tile):
            queries = qkv[0, row : row + tile, start : start + step] * jnp.asarray(SCALE, BF16)
            total, sums = None, None
            for head in range(step // HEAD_DIM):
                mask = head_mask(step, head)
                scores = dot(jnp.where(mask, queries, jnp.zeros_like(queries)), keys, (1, 1))
                top = jnp.max(scores, axis=1, keepdims=True)
                powers = jnp.exp(scores - top)
                weight = jnp.sum(powers, axis=1, keepdims=True)
                part = dot(powers.astype(BF16), values, (1, 0)) / weight
                level = jnp.broadcast_to(top + jnp.log(weight), part.shape)
                total = part if total is None else jnp.where(mask, part, total)
                sums = level if sums is None else jnp.where(mask, level, sums)
            out[0, row : row + tile, start : start + step] = total.astype(BF16)
            logsum[0, row : row + tile, start : start + step] = sums


def attend(qkv, width):
    latents, tokens, _ = qkv.shape
    spec = lambda columns: pl.BlockSpec((1, tokens, columns), lambda l: (l, 0, 0))
    return pl.pallas_call(
        partial(attend_kernel, width),
        grid=(latents,),
        in_specs=[spec(3 * width)],
        out_specs=[spec(width), spec(width)],
        out_shape=[
            jax.ShapeDtypeStruct((latents, tokens, width), BF16),
            jax.ShapeDtypeStruct((latents, tokens, width), F32),
        ],
        compiler_params=pltpu.CompilerParams(vmem_limit_bytes=VMEM_LIMIT),
        cost_estimate=pl.CostEstimate(
            flops=16 * latents * tokens * tokens * width,
            bytes_accessed=12 * latents * tokens * width,
            transcendentals=latents * tokens * tokens * width // HEAD_DIM,
        ),
    )(qkv)


def attend_back_kernel(width, qkv, grads, logsum, out, key_sum, value_sum):
    tokens = qkv.shape[1]
    step = min(128, width)
    tile = min(TILE, tokens)
    for start in range(0, width, step):
        keys = qkv[0, :, width + start : width + start + step]
        values = qkv[0, :, 2 * width + start : 2 * width + start + step]
        key_sum[...] = jnp.zeros_like(key_sum)
        value_sum[...] = jnp.zeros_like(value_sum)
        for row in range(0, tokens, tile):
            queries = qkv[0, row : row + tile, start : start + step] * jnp.asarray(SCALE, BF16)
            grad = grads[0, row : row + tile, start : start + step]
            query_grad = None
            for head in range(step // HEAD_DIM):
                mask = head_mask(step, head)
                own_queries = jnp.where(mask, queries, jnp.zeros_like(queries))
                own_grad = jnp.where(mask, grad, jnp.zeros_like(grad))
                lane = start + head * HEAD_DIM
                level = logsum[0, row : row + tile, lane : lane + 1]
                probs = jnp.exp(dot(own_queries, keys, (1, 1)) - level)
                prob_grad = dot(own_grad, values, (1, 1))
                inner = jnp.sum(probs * prob_grad, axis=1, keepdims=True)
                score_grad = (probs * (prob_grad - inner)).astype(BF16)
                part = dot(score_grad, keys, (1, 0))
                query_grad = part if query_grad is None else jnp.where(mask, part, query_grad)
                key_sum[...] += dot(score_grad, own_queries, (0, 0))
                value_sum[...] += dot(probs.astype(BF16), own_grad, (0, 0))
            out[0, row : row + tile, start : start + step] = (query_grad * SCALE).astype(BF16)
        out[0, :, width + start : width + start + step] = key_sum[...].astype(BF16)
        out[0, :, 2 * width + start : 2 * width + start + step] = value_sum[...].astype(BF16)


def attend_back(qkv, grads, logsum, width):
    latents, tokens, _ = qkv.shape
    step = min(128, width)
    spec = lambda columns: pl.BlockSpec((1, tokens, columns), lambda l: (l, 0, 0))
    return pl.pallas_call(
        partial(attend_back_kernel, width),
        grid=(latents,),
        in_specs=[spec(3 * width), spec(width), spec(width)],
        out_specs=spec(3 * width),
        out_shape=jax.ShapeDtypeStruct((latents, tokens, 3 * width), BF16),
        scratch_shapes=[pltpu.VMEM((tokens, step), F32), pltpu.VMEM((tokens, step), F32)],
        compiler_params=pltpu.CompilerParams(vmem_limit_bytes=VMEM_LIMIT),
        cost_estimate=pl.CostEstimate(
            flops=40 * latents * tokens * tokens * width,
            bytes_accessed=18 * latents * tokens * width,
            transcendentals=latents * tokens * tokens * width // HEAD_DIM,
        ),
    )(qkv, grads, logsum)


def local(
    grid,
    block_in,
    conditioning,
    cotangent,
    ada_weight,
    ada_bias,
    qkv_weight,
    qv_bias,
    out_weight,
    out_bias,
    up_weight,
    up_bias,
    down_weight,
    down_bias,
):
    grid.locate()
    size, at = grid.size, grid.at
    z_n, y_n, c_n, s_n = grid.shape
    _, rows, width = block_in.shape
    hidden = up_weight.shape[1]
    count = grid.count
    groups = c_n * s_n
    head_cols = width // groups
    short = width // count
    long = hidden // count
    block_cols = s_n * long
    half = hidden // 2
    own_group = at["c"] * s_n + at["s"]
    send = grid.send

    cond_own = conditioning[0].astype(F32)
    cond_act = jax.nn.silu(cond_own).astype(BF16)
    shares = jnp.concatenate([qv_bias, out_bias, up_bias, down_bias, cond_act])
    all_shares = lax.dynamic_update_slice(
        jnp.zeros((count, shares.shape[0]), BF16), shares[None], (grid.me, 0)
    )
    for name in ("c", "z", "y", "s"):
        all_shares = sum(grid.arrivals(all_shares, name))
    cuts = np.cumsum([qv_bias.shape[0], out_bias.shape[0], up_bias.shape[0]])
    bias_cols = shares.shape[0] - width
    b_qv, b_out, b_up, b_down = [
        part.reshape(-1).astype(F32) for part in jnp.split(all_shares[:, :bias_cols], cuts, axis=1)
    ]

    x_own = block_in[0]
    x_all = grid.gather(x_own, "s")
    cond_all = all_shares[:, bias_cols:].reshape(count // s_n, s_n, width)[:, 0]
    cond_flat = lax.dynamic_slice_in_dim(cond_all, grid.me * short, short, axis=1)
    bias_row = lax.dynamic_update_slice(
        jnp.zeros((6 * width,), F32), ada_bias.astype(F32), (grid.me * ada_bias.shape[0],)
    )
    terms = (dot(cond_flat, ada_weight, (1, 0)) + bias_row).reshape(z_n, y_n, c_n, 6 * width)
    modulation = grid.to_latents(terms)
    shift_attn, scale_attn, gate_attn, shift_mlp, scale_mlp, gate_mlp = jnp.split(modulation, 6)

    cols = qkv_weight.reshape(short, 3, groups, head_cols)
    blocks = []
    for c_d in range(c_n):
        for s_d in range(s_n):
            target = (at["c"] + c_d) % c_n * s_n + (at["s"] + s_d) % s_n
            part = lax.dynamic_index_in_dim(cols, target, 2, keepdims=False).reshape(short, 3 * head_cols)
            blocks.append(send(part, c=c_d, s=s_d) if c_d + s_d else part)
    value = jnp.concatenate([block[None] for block in blocks])
    parts, steps = grid.gather_rows(value, ("z", "y"))
    jobs, table = [], []
    for i, back in enumerate(steps):
        piece, block = divmod(i, z_n)
        for group, (c_d, s_d) in enumerate(np.ndindex(c_n, s_n)):
            jobs.append((piece, block * groups + group, 0, 0))
            table.append(grid.shard_of({**back, "c": c_d, "s": s_d}))
    w_qkv = place([part.reshape(-1, 1, short, 3 * head_cols) for part in parts], jobs, table)

    wide = half // width
    up_cols = up_weight.reshape(short, z_n * y_n, c_n, block_cols)
    up_own = lax.dynamic_index_in_dim(up_cols, at["c"], 2, keepdims=False).reshape(short, wide, width)
    up_other = lax.dynamic_index_in_dim(up_cols, 1 - at["c"], 2, keepdims=False).reshape(short, wide, width)
    up_other = send(up_other, c=1)
    units = [out_weight] + [rows_of[:, i] for rows_of in (up_own, up_other) for i in range(wide)]
    units = jnp.concatenate([unit[None] for unit in units])
    parts, steps = grid.gather_rows(units, ("z", "s", "y"))
    each = len(steps) // len(parts)
    jobs, table, out_jobs, out_table = [], [], [], []
    for i, back in enumerate(steps):
        piece, block = divmod(i, each)
        for c_d in range(c_n):
            shard = grid.shard_of({**back, "c": c_d})
            out_jobs.append((c_d, i, 0, 0))
            out_table.append(shard)
            for part in range(wide):
                jobs.append((piece, block, 1 + c_d * wide + part, part))
                table.append(shard)
    w_up = place(parts, jobs, table)
    out_own = jnp.concatenate([part[:, :1] for part in parts])
    w_out = place([out_own, send(out_own, c=1)], out_jobs, out_table)

    parts, steps = grid.gather_rows(down_weight[None], ("z", "y", "s"))
    jobs, table = [], []
    for i, back in enumerate(steps):
        shard = grid.shard_of(back)
        jobs.append(divmod(i, each) + (0, 0))
        table.append(shard // (c_n * s_n) * s_n + shard % s_n)
    w_down = place(parts, jobs, table)

    inputs = x_own.astype(F32)
    modded_all = modulate(x_all.astype(F32), shift_attn, scale_attn).astype(BF16)
    modded_all = modded_all.reshape(s_n * rows, width)
    modded_all = jnp.concatenate([modded_all, send(modded_all, c=1)])
    q_bias = lax.dynamic_index_in_dim(b_qv[:width].reshape(groups, head_cols), own_group, 0, keepdims=False)
    v_bias = lax.dynamic_index_in_dim(b_qv[width:].reshape(groups, head_cols), own_group, 0, keepdims=False)
    qkv_bias = jnp.concatenate([q_bias, jnp.zeros_like(q_bias), v_bias])
    qkv = (dot(modded_all, w_qkv, (1, 0)) + qkv_bias).astype(BF16).reshape(c_n, s_n * rows, 3 * head_cols)
    attended_all, logsum = attend(qkv, head_cols)

    parts = attended_all.reshape(c_n, s_n, rows, head_cols)
    arrived = []
    for c_d in range(c_n):
        for s_d in range(s_n):
            part = parts[c_d, s_d]
            arrived.append(send(part, c=-c_d, s=-s_d) if c_d + s_d else part)
    arrived = jnp.stack(arrived)
    ordered = []
    for c in range(c_n):
        for s in range(s_n):
            index = (c - at["c"]) % c_n * s_n + (s - at["s"]) % s_n
            ordered.append(lax.dynamic_index_in_dim(arrived, index, 0, keepdims=False))
    attended = jnp.concatenate(ordered, axis=1)
    attn_proj = dot(attended, w_out, (1, 0)) + b_out
    middle = inputs + gate_attn * attn_proj
    modded_mlp = modulate(middle, shift_mlp, scale_mlp).astype(BF16)
    mlp_all = jnp.concatenate([modded_mlp, send(modded_mlp, c=1)])
    up_half = lax.dynamic_index_in_dim(b_up.reshape(-1, c_n, block_cols), at["c"], 1, keepdims=False).reshape(half)
    pre_act = dot(mlp_all, w_up, (1, 0)) + up_half
    gelu_tanh = partial(jax.nn.gelu, approximate=True)
    activated = gelu_tanh(pre_act).astype(BF16)
    proj_terms = dot(activated, w_down, (1, 0))
    mlp_proj = proj_terms[:rows] + send(proj_terms[rows:], c=1) + b_down
    block_out = (middle + gate_mlp * mlp_proj).astype(BF16)

    out_cot = cotangent[0].astype(F32)
    mlp_grad = (gate_mlp * out_cot).astype(BF16)
    mlp_grad_all = jnp.concatenate([mlp_grad, send(mlp_grad, c=1)])
    down_bias_grad = jnp.sum(mlp_grad.astype(F32), axis=0)
    down_terms = dot(activated, mlp_grad_all, (0, 0), BF16).reshape(z_n, y_n, s_n, long, width)
    act_grad = dot(mlp_grad_all, w_down, (1, 1))
    _, gelu_back = jax.vjp(gelu_tanh, pre_act)
    pre_grad = gelu_back(act_grad)[0].astype(BF16)
    up_bias_grad = jnp.sum(pre_grad.astype(F32), axis=0)
    up_terms = dot(mlp_all, pre_grad, (0, 0), BF16).reshape(z_n, y_n, c_n, s_n, short, half)
    mod_terms = dot(pre_grad, w_up, (1, 1))
    mlp_mod_grad = mod_terms[:rows] + send(mod_terms[rows:].astype(BF16), c=1).astype(F32)
    _, mlp_mod_back = jax.vjp(modulate, middle, shift_mlp, scale_mlp)
    middle_part, shift_mlp_grad, scale_mlp_grad = mlp_mod_back(mlp_mod_grad)
    middle_grad = out_cot + middle_part
    gate_mlp_grad = jnp.sum(out_cot * mlp_proj, axis=0)
    attn_grad = (gate_attn * middle_grad).astype(BF16)
    gate_attn_grad = jnp.sum(middle_grad * attn_proj, axis=0)
    out_bias_grad = jnp.sum(attn_grad.astype(F32), axis=0)
    out_terms = dot(attended, attn_grad, (0, 0), BF16).reshape(z_n, y_n, c_n, s_n, short, width)
    attended_grad = dot(attn_grad, w_out, (1, 1), BF16).reshape(rows, groups, head_cols)
    arrived = []
    for c_d in range(c_n):
        for s_d in range(s_n):
            target = (at["c"] + c_d) % c_n * s_n + (at["s"] + s_d) % s_n
            part = lax.dynamic_index_in_dim(attended_grad, target, 1, keepdims=False)
            arrived.append(send(part, c=c_d, s=s_d) if c_d + s_d else part)
    grads_all = jnp.concatenate(arrived).reshape(c_n, s_n * rows, head_cols)
    qkv_grad = attend_back(qkv, grads_all, logsum, head_cols).reshape(c_n * s_n * rows, 3 * head_cols)
    qkv_terms = dot(modded_all, qkv_grad, (0, 0), BF16).reshape(z_n, y_n, c_n, s_n, short, 3 * head_cols)
    column_sums = jnp.sum(qkv_grad.astype(F32), axis=0)
    mod_terms = dot(qkv_grad, w_qkv, (1, 1)).reshape(c_n, s_n, rows, width)
    mod_sum = (mod_terms[0] + send(mod_terms[1].astype(BF16), c=1).astype(F32))
    attn_mod_grad = mod_sum[0]
    for d in range(1, s_n):
        attn_mod_grad = attn_mod_grad + send(mod_sum[d].astype(BF16), s=-d).astype(F32)
    _, attn_mod_back = jax.vjp(modulate, inputs, shift_attn, scale_attn)
    input_part, shift_attn_grad, scale_attn_grad = attn_mod_back(attn_mod_grad)
    input_grad = (middle_grad + input_part).astype(BF16)

    modulation_grad = jnp.concatenate(
        [shift_attn_grad, scale_attn_grad, gate_attn_grad, shift_mlp_grad, scale_mlp_grad, gate_mlp_grad]
    )
    def spread(value, index, n, axis):
        shape = value.shape[:axis] + (n,) + value.shape[axis:]
        start = tuple(index if i == axis else 0 for i in range(len(shape)))
        return lax.dynamic_update_slice(jnp.zeros(shape, F32), jnp.expand_dims(value, axis), start)

    q_sums = spread(column_sums[:head_cols], own_group, groups, 0).reshape(-1)
    v_sums = spread(column_sums[2 * head_cols :], own_group, groups, 0).reshape(-1)
    up_sums = spread(up_bias_grad.reshape(-1, block_cols), at["c"], c_n, 1).reshape(-1)
    total = jnp.concatenate([modulation_grad, q_sums, v_sums, out_bias_grad, up_sums, down_bias_grad])
    total = sum(grid.arrivals(total, "s"))
    for name in ("z", "y", "c"):
        total = grid.gather(total, name)
    z, y, c = (
        (at[name] - jnp.arange(size[name])) % size[name] for name in ("z", "y", "c")
    )
    latent = ((z[None, None] * y_n + y[None, :, None]) * c_n + c[:, None, None]).reshape(-1)
    cond_back = jnp.dot(jax.nn.one_hot(latent, count // s_n, dtype=BF16), cond_flat, preferred_element_type=F32)
    mod_grads = total.reshape(-1, total.shape[-1])[:, : 6 * width]
    bias_sums = jnp.sum(total.reshape(-1, total.shape[-1]), axis=0)

    def own_share(start, kept):
        return lax.dynamic_slice_in_dim(bias_sums[start : start + kept * count], grid.me * kept, kept)

    ada_bias_grad = own_share(0, ada_bias.shape[0])
    start = 6 * width
    bias_grads = []
    for bias in (qv_bias, out_bias, up_bias, down_bias):
        bias_grads.append(own_share(start, bias.shape[0]))
        start += bias.shape[0] * count
    qv_bias_grad, out_bias_grad, up_bias_grad, down_bias_grad = bias_grads
    ada_weight_grad = lax.dot_general(
        cond_back, mod_grads, (((0,), (0,)), ((), ())), precision=HIGHEST
    )
    cond_terms = lax.dot_general(
        mod_grads, ada_weight.astype(F32), (((1,), (1,)), ((), ())), precision=HIGHEST
    )
    cond_terms = lax.dynamic_update_slice(
        jnp.zeros((cond_terms.shape[0], width), F32), cond_terms, (0, grid.me * short)
    )
    cond_terms = cond_terms.reshape(c_n, y_n, z_n, width)
    for name in ("c", "y", "z"):
        moved = [cond_terms[0]] + [send(cond_terms[d], **{name: -d}) for d in range(1, size[name])]
        cond_terms = sum(moved)
    cond_total = sum(grid.arrivals(cond_terms, "s"))
    _, silu_back = jax.vjp(jax.nn.silu, cond_own)
    cond_grad = silu_back(cond_total)[0].astype(BF16)[None]

    for axis, name in ((1, "y"), (1, "s"), (0, "z")):
        down_terms = grid.reduce(down_terms, axis, name, F32 if name == "z" else BF16)
    down_weight_grad = down_terms
    out_terms = grid.reduce(out_terms, 2, "c", BF16)
    up_first = lax.dynamic_index_in_dim(up_terms, at["c"], 2, keepdims=False)
    up_second = lax.dynamic_index_in_dim(up_terms, 1 - at["c"], 2, keepdims=False)
    units = [out_terms] + [
        rows_of[..., i * width : (i + 1) * width] for rows_of in (up_first, up_second) for i in range(wide)
    ]
    units = jnp.concatenate(units, axis=3)
    for axis, name in ((2, "s"), (1, "y"), (0, "z")):
        units = grid.reduce(units, axis, name, F32 if name == "z" else BF16)
    units = units.reshape(1 + c_n * wide, short, width)
    out_weight_grad = units[0]
    up_first, up_second = [
        jnp.concatenate([units[first + i] for i in range(wide)], axis=1).reshape(short, -1, 1, block_cols)
        for first in (1, 1 + wide)
    ]
    up_second = send(up_second, c=1)
    even = at["c"] == 0
    up_weight_grad = jnp.concatenate(
        [jnp.where(even, up_first, up_second), jnp.where(even, up_second, up_first)], axis=2
    ).reshape(short, hidden)
    qkv_terms = grid.reduce(grid.reduce(qkv_terms, 1, "y", BF16), 0, "z", F32)
    qkv_terms = qkv_terms.reshape(groups, short, 3 * head_cols)
    arrived = []
    for c_d in range(c_n):
        for s_d in range(s_n):
            target = (at["c"] + c_d) % c_n * s_n + (at["s"] + s_d) % s_n
            part = lax.dynamic_index_in_dim(qkv_terms, target, 0, keepdims=False)
            arrived.append(send(part, c=c_d, s=s_d) if c_d + s_d else part)
    arrived = jnp.stack(arrived)
    ordered = []
    for c in range(c_n):
        for s in range(s_n):
            index = (at["c"] - c) % c_n * s_n + (at["s"] - s) % s_n
            ordered.append(lax.dynamic_index_in_dim(arrived, index, 0, keepdims=False).reshape(short, 3, head_cols))
    qkv_weight_grad = jnp.stack(ordered, axis=2).reshape(short, 3 * width)

    return (
        block_out[None],
        input_grad[None],
        cond_grad,
        ada_weight_grad,
        ada_bias_grad,
        qkv_weight_grad,
        qv_bias_grad,
        out_weight_grad,
        out_bias_grad,
        up_weight_grad,
        up_bias_grad,
        down_weight_grad,
        down_bias_grad,
    )


def solution(mesh):
    tokens = P("batch", "seq", None)
    vector = P("batch", None)
    matrix, line = P(AXES, None), P(AXES)
    in_specs = (tokens, vector, tokens) + (matrix, line) * 5
    out_specs = (tokens, tokens, vector) + (matrix, line) * 5
    return jax.shard_map(
        partial(local, Grid(mesh)), mesh=mesh, in_specs=in_specs, out_specs=out_specs, check_vma=False
    )
```

```python
from functools import partial

import jax
import jax.numpy as jnp
import numpy as np
from jax import lax
from jax.experimental import pallas as pl
from jax.experimental.pallas import tpu as pltpu
from jax.sharding import PartitionSpec as P

HEAD_DIM = 64
SCALE = HEAD_DIM**-0.5
EPSILON = 1e-06
HIGHEST = lax.Precision.HIGHEST
F32, BF16 = jnp.float32, jnp.bfloat16
AXES = ("batch", "seq")
VMEM_LIMIT = 56 * 1024 * 1024
TILE = 256


def dot(left, right, dims, kind=F32):
    out = lax.dot_general(left, right, ((dims[:1], dims[1:]), ((), ())), preferred_element_type=F32)
    return out.astype(kind)


def after(value, *needed):
    return lax.optimization_barrier((value,) + needed)[0]


def settle(parts, kind, *needed):
    if needed:
        parts = lax.optimization_barrier(tuple(parts) + needed)[: len(parts)]
    return sum(part.astype(F32) for part in parts).astype(kind)


def normalize(values):
    average = jnp.mean(values, axis=-1, keepdims=True)
    centered = values - average
    variance = jnp.mean(centered * centered, axis=-1, keepdims=True)
    inverse = lax.rsqrt(variance + EPSILON)
    return centered * inverse, inverse


def normalize_back(grads, normed, inverse):
    average = jnp.mean(grads, axis=-1, keepdims=True)
    along = jnp.mean(grads * normed, axis=-1, keepdims=True)
    return inverse * (grads - average - normed * along)


class Grid:
    def __init__(self, mesh):
        batch, seq = mesh.shape["batch"], mesh.shape["seq"]
        self.size = {"z": batch // 4, "y": 2, "c": 2, "s": seq}
        self.shape = tuple(self.size.values())
        self.count = batch * seq

    def locate(self):
        batch, seq = lax.axis_index("batch"), lax.axis_index("seq")
        self.at = {"z": batch // 4, "y": (batch // 2) % 2, "c": batch % 2, "s": seq}
        self.me = batch * self.size["s"] + seq

    def send(self, value, **steps):
        moves = [steps.get(name, 0) for name in self.size]
        pairs = []
        for place in np.ndindex(*self.shape):
            target = tuple((p + m) % n for p, m, n in zip(place, moves, self.shape))
            pairs.append(
                (int(np.ravel_multi_index(place, self.shape)), int(np.ravel_multi_index(target, self.shape)))
            )
        return lax.ppermute(value, AXES, pairs)

    def steps(self, *names):
        return [dict(zip(names, at)) for at in np.ndindex(*[self.size[name] for name in names])]

    def arrivals(self, value, *names):
        return [self.send(value, **step) if any(step.values()) else value for step in self.steps(*names)]

    def gather(self, value, *names):
        return jnp.concatenate([part[None] for part in self.arrivals(value, *names)])

    def shed(self, terms, axis, name):
        n, me = self.size[name], self.at[name]
        parts = [lax.dynamic_index_in_dim(terms, (me + d) % n, axis, keepdims=False) for d in range(n)]
        self.sent = parts[1:]
        return [self.send(part, **{name: d}) if d else part for d, part in enumerate(parts)]

    def reduce(self, terms, axis, name, kind):
        return settle(self.shed(terms, axis, name), kind)

    def shard_of(self, back):
        index = 0
        for name, n in self.size.items():
            index = index * n + (self.at[name] - back.get(name, 0)) % n
        return index

    def sum_over(self, value, *names):
        return sum(self.arrivals(value, *names))


def place_kernel(jobs, flat, table, *refs):
    pieces, out, sems = refs[:-2], refs[-2], refs[-1]
    copies = []
    for at, (piece, block, unit, part) in enumerate(jobs):
        source = pieces[piece].at[block, unit]
        rows, columns = source.shape
        if flat:
            target = out.at[
                pl.ds(pl.multiple_of(table[at] * rows, rows), rows), pl.ds(part * columns, columns)
            ]
        else:
            target = out.at[table[at], part]
        copies.append(pltpu.make_async_copy(source, target, sems.at[at]))
        copies[-1].start()
    for copy in copies:
        copy.wait()


def place(pieces, jobs, table):
    rows, columns = pieces[0].shape[2:]
    parts = 1 + max(job[3] for job in jobs)
    count = len(jobs) // parts
    flat = rows % 16 == 0
    out = pl.pallas_call(
        partial(place_kernel, jobs, flat),
        out_shape=jax.ShapeDtypeStruct(
            (count * rows, parts * columns) if flat else (count, parts, rows, columns), pieces[0].dtype
        ),
        grid_spec=pltpu.PrefetchScalarGridSpec(
            num_scalar_prefetch=1,
            in_specs=[pl.BlockSpec(memory_space=pl.ANY)] * len(pieces),
            out_specs=pl.BlockSpec(memory_space=pltpu.VMEM if flat else pl.ANY),
            scratch_shapes=[pltpu.SemaphoreType.DMA((len(jobs),))],
        ),
        compiler_params=pltpu.CompilerParams(vmem_limit_bytes=VMEM_LIMIT),
        cost_estimate=pl.CostEstimate(
            flops=0, bytes_accessed=4 * len(jobs) * rows * columns, transcendentals=0
        ),
    )(jnp.stack(table).astype(jnp.int32), *pieces)
    if not flat:
        out = out.transpose(0, 2, 1, 3).reshape(count * rows, parts * columns)
    return out


def columns_kernel(width, table, *refs):
    pieces, out = refs[:-1], refs[-1]
    total = out.shape[1] // 3
    for at, piece in enumerate(pieces):
        for part in range(3):
            start = pl.multiple_of(part * total + table[at] * width, width)
            out[:, pl.ds(start, width)] = piece[:, part * width : (part + 1) * width]


def place_columns(pieces, table, width):
    rows, total = pieces[0].shape[0], len(pieces) * 3 * width
    if width % 128 != 0:
        out = jnp.zeros((rows, 3, total // 3), F32)
        for piece, group in zip(pieces, table):
            out = lax.dynamic_update_slice(out, piece.reshape(rows, 3, width), (0, 0, group * width))
        return out.reshape(rows, total)
    return pl.pallas_call(
        partial(columns_kernel, width),
        out_shape=jax.ShapeDtypeStruct((rows, total), F32),
        grid_spec=pltpu.PrefetchScalarGridSpec(
            num_scalar_prefetch=1,
            in_specs=[pl.BlockSpec(memory_space=pltpu.VMEM)] * len(pieces),
            out_specs=pl.BlockSpec(memory_space=pltpu.VMEM),
        ),
    )(jnp.stack(table).astype(jnp.int32), *pieces)


def head_mask(width, head):
    lanes = lax.broadcasted_iota(jnp.int32, (1, width), 1)
    return (lanes >= head * HEAD_DIM) & (lanes < (head + 1) * HEAD_DIM)


def attend_kernel(width, qkv, out, logsum):
    tokens = qkv.shape[1]
    step = min(128, width)
    tile = min(TILE, tokens)
    for start in range(0, width, step):
        keys = qkv[0, :, width + start : width + start + step]
        values = qkv[0, :, 2 * width + start : 2 * width + start + step]
        for row in range(0, tokens, tile):
            queries = qkv[0, row : row + tile, start : start + step] * jnp.asarray(SCALE, BF16)
            total, sums = None, None
            for head in range(step // HEAD_DIM):
                mask = head_mask(step, head)
                scores = dot(jnp.where(mask, queries, jnp.zeros_like(queries)), keys, (1, 1))
                top = jnp.max(scores, axis=1, keepdims=True)
                powers = jnp.exp(scores - top)
                weight = jnp.sum(powers, axis=1, keepdims=True)
                part = dot(powers.astype(BF16), values, (1, 0)) / weight
                level = jnp.broadcast_to(top + jnp.log(weight), part.shape)
                total = part if total is None else jnp.where(mask, part, total)
                sums = level if sums is None else jnp.where(mask, level, sums)
            out[0, row : row + tile, start : start + step] = total.astype(BF16)
            logsum[0, row : row + tile, start : start + step] = sums


def attend(qkv, latent, width):
    _, tokens, _ = qkv.shape
    spec = lambda columns, at: pl.BlockSpec((1, tokens, columns), lambda l: (at, 0, 0))
    return pl.pallas_call(
        partial(attend_kernel, width),
        grid=(1,),
        in_specs=[spec(3 * width, latent)],
        out_specs=[spec(width, 0), spec(width, 0)],
        out_shape=[
            jax.ShapeDtypeStruct((1, tokens, width), BF16),
            jax.ShapeDtypeStruct((1, tokens, width), F32),
        ],
        compiler_params=pltpu.CompilerParams(vmem_limit_bytes=VMEM_LIMIT),
        cost_estimate=pl.CostEstimate(
            flops=tokens * tokens * width,
            bytes_accessed=12 * tokens * width,
            transcendentals=0,
        ),
    )(qkv)


def attend_back_kernel(width, qkv, grads, logsum, out, key_sum, value_sum):
    tokens = qkv.shape[1]
    step = min(128, width)
    tile = min(TILE, tokens)
    for start in range(0, width, step):
        keys = qkv[0, :, width + start : width + start + step]
        values = qkv[0, :, 2 * width + start : 2 * width + start + step]
        key_sum[...] = jnp.zeros_like(key_sum)
        value_sum[...] = jnp.zeros_like(value_sum)
        for row in range(0, tokens, tile):
            queries = qkv[0, row : row + tile, start : start + step] * jnp.asarray(SCALE, BF16)
            grad = grads[0, row : row + tile, start : start + step]
            query_grad = None
            for head in range(step // HEAD_DIM):
                mask = head_mask(step, head)
                own_queries = jnp.where(mask, queries, jnp.zeros_like(queries))
                own_grad = jnp.where(mask, grad, jnp.zeros_like(grad))
                lane = start + head * HEAD_DIM
                level = logsum[0, row : row + tile, lane : lane + 1]
                probs = jnp.exp(dot(own_queries, keys, (1, 1)) - level)
                prob_grad = dot(own_grad, values, (1, 1))
                inner = jnp.sum(probs * prob_grad, axis=1, keepdims=True)
                score_grad = (probs * (prob_grad - inner)).astype(BF16)
                part = dot(score_grad, keys, (1, 0))
                query_grad = part if query_grad is None else jnp.where(mask, part, query_grad)
                key_sum[...] += dot(score_grad, own_queries, (0, 0))
                value_sum[...] += dot(probs.astype(BF16), own_grad, (0, 0))
            out[0, row : row + tile, start : start + step] = (query_grad * SCALE).astype(BF16)
        out[0, :, width + start : width + start + step] = key_sum[...].astype(BF16)
        out[0, :, 2 * width + start : 2 * width + start + step] = value_sum[...].astype(BF16)


def attend_back(qkv, grads, logsum, latent, width):
    _, tokens, _ = qkv.shape
    step = min(128, width)
    spec = lambda columns, at: pl.BlockSpec((1, tokens, columns), lambda l: (at, 0, 0))
    return pl.pallas_call(
        partial(attend_back_kernel, width),
        grid=(1,),
        in_specs=[spec(3 * width, latent), spec(width, 0), spec(width, 0)],
        out_specs=spec(3 * width, 0),
        out_shape=jax.ShapeDtypeStruct((1, tokens, 3 * width), BF16),
        scratch_shapes=[pltpu.VMEM((tokens, step), F32), pltpu.VMEM((tokens, step), F32)],
        compiler_params=pltpu.CompilerParams(vmem_limit_bytes=VMEM_LIMIT),
        cost_estimate=pl.CostEstimate(
            flops=2 * tokens * tokens * width,
            bytes_accessed=18 * tokens * width,
            transcendentals=0,
        ),
    )(qkv, grads, logsum)


def local(
    grid,
    block_in,
    conditioning,
    cotangent,
    ada_weight,
    ada_bias,
    qkv_weight,
    qv_bias,
    out_weight,
    out_bias,
    up_weight,
    up_bias,
    down_weight,
    down_bias,
):
    grid.locate()
    size, at = grid.size, grid.at
    z_n, y_n, c_n, s_n = grid.shape
    _, rows, width = block_in.shape
    hidden = up_weight.shape[1]
    count = grid.count
    groups = c_n * s_n
    head_cols = width // groups
    short = width // count
    long = hidden // count
    block_cols = s_n * long
    half = hidden // 2
    own_group = at["c"] * s_n + at["s"]
    send = grid.send

    cond_own = conditioning[0].astype(F32)
    cond_act = jax.nn.silu(cond_own).astype(BF16)
    shares = jnp.concatenate([qv_bias, out_bias, up_bias, down_bias, cond_act])
    cols = qkv_weight.reshape(short, 3, groups, head_cols)
    blocks = []
    for c_d, s_d in np.ndindex(c_n, s_n):
        target = (at["c"] + c_d) % c_n * s_n + (at["s"] + s_d) % s_n
        part = lax.dynamic_index_in_dim(cols, target, 2, keepdims=False).reshape(short, 3 * head_cols)
        blocks.append(send(part, c=c_d, s=s_d) if c_d + s_d else part)
    x_own = block_in[0]
    shares = after(jnp.broadcast_to(shares[None], (count,) + shares.shape), *blocks)
    qkv_z = grid.gather(jnp.concatenate([block[None] for block in blocks]), "z")
    all_shares = lax.all_to_all(shares, AXES, 0, 0, tiled=True)
    x_all = grid.gather(after(x_own, all_shares), "s")
    cuts = np.cumsum([qv_bias.shape[0], out_bias.shape[0], up_bias.shape[0]])
    bias_cols = shares.shape[1] - width
    b_qv, b_out, b_up, b_down = [
        part.reshape(-1).astype(F32) for part in jnp.split(all_shares[:, :bias_cols], cuts, axis=1)
    ]

    cond_all = all_shares[:, bias_cols:].reshape(count // s_n, s_n, width)[:, 0]
    cond_flat = lax.dynamic_slice_in_dim(cond_all, grid.me * short, short, axis=1)
    bias_row = lax.dynamic_update_slice(
        jnp.zeros((6 * width,), F32), ada_bias.astype(F32), (grid.me * ada_bias.shape[0],)
    )
    terms = (dot(cond_flat, ada_weight, (1, 0)) + bias_row).reshape(count, 6 * width // s_n)
    terms = lax.all_to_all(after(terms, qkv_z), AXES, 0, 0, tiled=True)
    small_z = terms
    parts = grid.arrivals(after(qkv_z, terms), "y")
    terms = grid.gather(jnp.sum(terms, axis=0), "s")
    modulation = jnp.concatenate(
        [lax.dynamic_index_in_dim(terms, (at["s"] - s) % s_n, 0, keepdims=False) for s in range(s_n)]
    )
    shift_attn, scale_attn, gate_attn, shift_mlp, scale_mlp, gate_mlp = jnp.split(modulation, 6)

    jobs, table = [], []
    for i, back in enumerate(grid.steps("y", "z")):
        piece, block = divmod(i, z_n)
        for group, (c_d, s_d) in enumerate(np.ndindex(c_n, s_n)):
            jobs.append((piece, block * groups + group, 0, 0))
            table.append(grid.shard_of({**back, "c": c_d, "s": s_d}))
    w_qkv = place([part.reshape(-1, 1, short, 3 * head_cols) for part in parts], jobs, table)

    wide = half // width
    up_cols = up_weight.reshape(short, z_n * y_n, c_n, block_cols)
    up_own = lax.dynamic_index_in_dim(up_cols, at["c"], 2, keepdims=False).reshape(short, wide, width)
    up_other = lax.dynamic_index_in_dim(up_cols, 1 - at["c"], 2, keepdims=False).reshape(short, wide, width)
    up_other = send(after(up_other, x_all), c=1)
    units = [out_weight] + [rows_of[:, i] for rows_of in (up_own, up_other) for i in range(wide)]
    units = jnp.concatenate([unit[None] for unit in units])
    orders = (("s", "y"), ("y", "s"))
    units_z = grid.arrivals(after(units, small_z), "z")
    up_first = [
        grid.gather(jnp.concatenate([part[None, low:high] for part in units_z]), order[0])
        for low, high, order in ((0, 1 + wide, orders[0]), (1 + wide, 1 + 2 * wide, orders[1]))
    ]
    down_z = grid.arrivals(after(down_weight.reshape(2, long // 2, width), *up_first), "z")
    up_last = [grid.arrivals(after(part, *up_first), order[1]) for part, order in zip(up_first, orders)]
    down_first = [
        grid.gather(jnp.concatenate([part[None, i : i + 1] for part in down_z]), order[0])
        for i, order in enumerate(orders)
    ]

    inputs = x_own.astype(F32)
    normed_all, inverse_all = normalize(x_all.astype(F32))
    modded_all = (normed_all * (1.0 + scale_attn) + shift_attn).astype(BF16).reshape(s_n * rows, width)
    modded_all = jnp.concatenate([modded_all, send(modded_all, c=1)])
    q_bias = lax.dynamic_index_in_dim(b_qv[:width].reshape(groups, head_cols), own_group, 0, keepdims=False)
    v_bias = lax.dynamic_index_in_dim(b_qv[width:].reshape(groups, head_cols), own_group, 0, keepdims=False)
    qkv_bias = jnp.concatenate([q_bias, jnp.zeros_like(q_bias), v_bias])
    qkv = (dot(modded_all, w_qkv, (1, 0)) + qkv_bias).astype(BF16).reshape(c_n, s_n * rows, 3 * head_cols)
    attended_all, logsums = [], []
    for latent in range(c_n):
        qkv = after(qkv, *(attended_all + down_z if latent else up_first))
        part, logsum = attend(qkv, latent, head_cols)
        attended_all.append(part.reshape(s_n, rows, head_cols))
        logsums.append(logsum)
    arrived = []
    for c_d, s_d in np.ndindex(c_n, s_n):
        part = attended_all[c_d][s_d]
        if c_d + s_d:
            part = after(part, *attended_all)
        arrived.append(send(part, c=-c_d, s=-s_d) if c_d + s_d else part)
    up_steps = [grid.steps(order[1], order[0], "z") for order in orders]
    each = count // (c_n * grid.size["y"])
    flat_last = lax.optimization_barrier(tuple(part for parts in up_last for part in parts) + tuple(arrived))
    arrived = flat_last[-len(arrived) :]
    parts = [part.reshape((-1,) + part.shape[2:]) for part in flat_last[: -len(arrived)]]
    jobs, table, out_jobs, out_table = [], [], [], []
    first = 0
    for c_d, (last, steps) in enumerate(zip(up_last, up_steps)):
        per = len(steps) // len(last)
        for i, back in enumerate(steps):
            piece, block = divmod(i, per)
            for part in range(wide):
                jobs.append((first + piece, block, part + 1 - c_d, part))
                table.append(grid.shard_of({**back, "c": c_d}))
        first += len(last)
    out_own = jnp.concatenate([part[:, :1] for part in parts[: len(up_last[0])]])
    for c_d in range(c_n):
        for i, back in enumerate(up_steps[0]):
            out_jobs.append((c_d, i, 0, 0))
            out_table.append(grid.shard_of({**back, "c": c_d}))
    w_out = place([out_own, send(out_own, c=1)], out_jobs, out_table)
    w_up = place(parts, jobs, table)
    arrived = jnp.stack(arrived)
    ordered = []
    for c in range(c_n):
        for s in range(s_n):
            index = (c - at["c"]) % c_n * s_n + (s - at["s"]) % s_n
            ordered.append(lax.dynamic_index_in_dim(arrived, index, 0, keepdims=False))
    attended = jnp.concatenate(ordered, axis=1)
    attn_proj = dot(attended, w_out, (1, 0)) + b_out
    middle = inputs + gate_attn * attn_proj
    normed_mid, inverse_mid = normalize(middle)
    modded_mlp = (normed_mid * (1.0 + scale_mlp) + shift_mlp).astype(BF16)
    mlp_all = jnp.concatenate([modded_mlp, send(modded_mlp, c=1)])
    up_half = lax.dynamic_index_in_dim(b_up.reshape(-1, c_n, block_cols), at["c"], 1, keepdims=False).reshape(half)
    mlp_all = after(mlp_all, *down_first)
    down_last = [grid.arrivals(part, order[1]) for part, order in zip(down_first, orders)]
    pre_act = dot(mlp_all, w_up, (1, 0)) + up_half
    gelu_tanh = partial(jax.nn.gelu, approximate=True)
    activated = gelu_tanh(pre_act).astype(BF16)
    out_cot = cotangent[0].astype(F32)
    mlp_grad = (gate_mlp * out_cot).astype(BF16)
    mlp_grad_all = jnp.concatenate([mlp_grad, send(mlp_grad, c=1)])
    down_terms = dot(activated, mlp_grad_all, (0, 0), BF16).reshape(z_n, y_n, s_n, long, width)
    flat_last = lax.optimization_barrier((down_terms,) + tuple(part for parts in down_last for part in parts))
    down_terms = flat_last[0]
    down_a = grid.shed(down_terms[..., : long // 2, :], 2, "s")
    down_sent = grid.sent
    down_b = grid.shed(down_terms[..., long // 2 :, :], 1, "y")
    down_sent = down_sent + grid.sent
    parts = [part.reshape((-1,) + part.shape[2:]) for part in flat_last[1:]]
    jobs, table = [], []
    first = 0
    for row_half, (last, order) in enumerate(zip(down_last, orders)):
        steps = grid.steps(order[1], order[0], "z")
        per = len(steps) // len(last)
        for i, back in enumerate(steps):
            shard = grid.shard_of(back)
            piece, block = divmod(i, per)
            jobs.append((first + piece, block, 0, 0))
            table.append((shard // (c_n * s_n) * s_n + shard % s_n) * 2 + row_half)
        first += len(last)
    w_down = place(parts, jobs, table)
    proj_terms = dot(activated, w_down, (1, 0))
    mlp_proj = proj_terms[:rows] + send(proj_terms[rows:], c=1) + b_down
    block_out = (middle + gate_mlp * mlp_proj).astype(BF16)

    down_bias_grad = jnp.sum(mlp_grad.astype(F32), axis=0)
    act_grad = dot(after(mlp_grad_all, proj_terms, *down_sent), w_down, (1, 1))
    _, gelu_back = jax.vjp(gelu_tanh, pre_act)
    pre_grad = gelu_back(act_grad)[0].astype(BF16)
    up_bias_grad = jnp.sum(pre_grad.astype(F32), axis=0)
    down_a, down_b = settle(down_a, BF16, pre_grad), settle(down_b, BF16, pre_grad)
    up_terms = dot(after(mlp_all, down_a, down_b), pre_grad, (0, 0), BF16)
    up_terms = up_terms.reshape(z_n, y_n, c_n, s_n, short, half)
    up_a = grid.shed(lax.dynamic_index_in_dim(up_terms, at["c"], 2, keepdims=False), 1, "y")
    up_sent = grid.sent
    up_b = grid.shed(lax.dynamic_index_in_dim(up_terms, 1 - at["c"], 2, keepdims=False), 2, "s")
    up_sent = up_sent + grid.sent
    down_a, down_b = grid.shed(down_a, 1, "y"), grid.shed(down_b, 1, "s")
    mod_terms = dot(after(pre_grad, *up_sent), w_up, (1, 1))
    mlp_mod_grad = mod_terms[:rows] + send(mod_terms[rows:].astype(BF16), c=1).astype(F32)
    middle_part = normalize_back(mlp_mod_grad * (1.0 + scale_mlp), normed_mid, inverse_mid)
    shift_mlp_grad = jnp.sum(mlp_mod_grad, axis=0)
    scale_mlp_grad = jnp.sum(mlp_mod_grad * normed_mid, axis=0)
    middle_grad = out_cot + middle_part
    gate_mlp_grad = jnp.sum(out_cot * mlp_proj, axis=0)
    attn_grad = (gate_attn * middle_grad).astype(BF16)
    down_terms = jnp.concatenate([settle(part, BF16, attn_grad) for part in (down_a, down_b)], axis=1)
    up_a, up_b = settle(up_a, BF16, attn_grad), settle(up_b, BF16, attn_grad)
    attn_grad = after(attn_grad, down_terms, up_a, up_b)
    gate_attn_grad = jnp.sum(middle_grad * attn_proj, axis=0)
    out_bias_grad = jnp.sum(attn_grad.astype(F32), axis=0)
    attended_grad = dot(attn_grad, w_out, (1, 1), BF16)
    arrived = []
    for c_d in range(c_n):
        for s_d in range(s_n):
            target = (at["c"] + c_d) % c_n * s_n + (at["s"] + s_d) % s_n
            part = lax.dynamic_slice_in_dim(attended_grad, target * head_cols, head_cols, axis=1)
            arrived.append(send(part, c=c_d, s=s_d) if c_d + s_d else part)
    up_a, up_b = after(up_a, *arrived), after(up_b, *arrived)
    up_a, up_b = grid.shed(up_a, 1, "s"), grid.shed(up_b, 1, "y")
    down_terms = grid.shed(down_terms, 0, "z")
    out_terms = dot(attended, after(attn_grad, attended_grad), (0, 0), BF16)
    out_terms = out_terms.reshape(z_n, y_n, c_n, s_n, short, width)
    out_terms = grid.reduce(out_terms, 2, "c", BF16)
    up_terms = jnp.concatenate([settle(part, BF16, out_terms) for part in (up_a, up_b)], axis=1)
    out_terms = grid.shed(out_terms, 2, "s")
    out_sent = grid.sent
    up_terms = grid.shed(after(up_terms, *out_sent), 0, "z")
    up_sent = grid.sent
    qkv_grads = []
    for latent in range(c_n):
        grads = jnp.concatenate(arrived[latent * s_n : (latent + 1) * s_n])[None]
        if latent == 0:
            grads = after(grads, *out_sent, *up_sent)
        else:
            down_weight_grad = settle(down_terms, F32, *qkv_grads)
            out_terms = grid.shed(settle(out_terms, BF16, *qkv_grads), 1, "y")
            grads = after(grads, down_weight_grad, *grid.sent)
        qkv_grads.append(attend_back(qkv, grads, logsums[latent], latent, head_cols))
    qkv_grad = jnp.concatenate(qkv_grads).reshape(c_n * s_n * rows, 3 * head_cols)
    up_terms = settle(up_terms, F32, qkv_grad)
    out_terms = grid.shed(settle(out_terms, BF16, qkv_grad), 0, "z")
    qkv_grad = after(qkv_grad, up_terms, *grid.sent)
    mod_terms = dot(qkv_grad, w_qkv, (1, 1)).reshape(c_n, s_n, rows, width)
    mod_sent = mod_terms[1].astype(BF16)
    qkv_terms = dot(modded_all, after(qkv_grad, mod_sent), (0, 0), BF16)
    qkv_terms = qkv_terms.reshape(z_n, y_n, c_n, s_n, short, 3 * head_cols)
    qkv_terms = grid.shed(qkv_terms, 1, "y")
    out_weight_grad = settle(out_terms, F32, *grid.sent)
    mod_terms = after(mod_terms[0], out_weight_grad, *grid.sent)
    mod_sum = mod_terms + send(mod_sent, c=1).astype(F32)
    shift_attn_grad = jnp.sum(mod_sum, axis=(0, 1))
    scale_attn_grad = jnp.sum(mod_sum * normed_all, axis=(0, 1))
    column_sums = jnp.sum(qkv_grad.astype(F32), axis=0)
    arrived = [send(mod_sum[d].astype(BF16), s=-d) for d in range(1, s_n)]

    modulation_grad = jnp.concatenate(
        [shift_attn_grad, scale_attn_grad, gate_attn_grad, shift_mlp_grad, scale_mlp_grad, gate_mlp_grad]
    )
    def spread(value, index, n, axis):
        shape = value.shape[:axis] + (n,) + value.shape[axis:]
        start = tuple(index if i == axis else 0 for i in range(len(shape)))
        return lax.dynamic_update_slice(jnp.zeros(shape, F32), jnp.expand_dims(value, axis), start)

    q_sums = spread(column_sums[:head_cols], own_group, groups, 0).reshape(-1)
    v_sums = spread(column_sums[2 * head_cols :], own_group, groups, 0).reshape(-1)
    up_sums = spread(up_bias_grad.reshape(-1, block_cols), at["c"], c_n, 1).reshape(-1)
    total = jnp.concatenate([modulation_grad, q_sums, v_sums, out_bias_grad, up_sums, down_bias_grad])
    total = grid.sum_over(total, "s")
    total = grid.gather(total, "z")
    qkv_terms = settle(qkv_terms, BF16, total)
    qkv_terms = grid.shed(qkv_terms, 0, "z")
    total = grid.gather(after(total, *grid.sent), "c", "y")
    attn_mod_grad = mod_sum[0]
    for part in arrived:
        attn_mod_grad = attn_mod_grad + after(part, total).astype(F32)
    input_part = normalize_back(attn_mod_grad * (1.0 + scale_attn), normed_all[0], inverse_all[0])
    input_grad = (middle_grad + input_part).astype(BF16)
    z, y, c = ((at[name] - jnp.arange(size[name])) % size[name] for name in ("z", "y", "c"))
    latent = ((z[None, None] * y_n + y[None, :, None]) * c_n + c[:, None, None]).reshape(-1)
    cond_back = jnp.dot(jax.nn.one_hot(latent, count // s_n, dtype=BF16), cond_flat, preferred_element_type=F32)
    mod_grads = total.reshape(-1, total.shape[-1])[:, : 6 * width]
    bias_sums = jnp.sum(total.reshape(-1, total.shape[-1]), axis=0)

    def own_share(start, kept):
        return lax.dynamic_slice_in_dim(bias_sums[start : start + kept * count], grid.me * kept, kept)

    ada_bias_grad = own_share(0, ada_bias.shape[0])
    start = 6 * width
    bias_grads = []
    for bias in (qv_bias, out_bias, up_bias, down_bias):
        bias_grads.append(own_share(start, bias.shape[0]))
        start += bias.shape[0] * count
    qv_bias_grad, out_bias_grad, up_bias_grad, down_bias_grad = bias_grads
    ada_weight_grad = lax.dot_general(
        cond_back, mod_grads, (((0,), (0,)), ((), ())), precision=HIGHEST
    )
    cond_terms = lax.dot_general(
        mod_grads, ada_weight.astype(F32), (((1,), (1,)), ((), ())), precision=HIGHEST
    )
    cond_terms = after(cond_terms, input_grad)
    order = (latent[:, None] == jnp.arange(count // s_n)[None]).astype(F32)
    cond_terms = lax.dot_general(order, cond_terms, (((0,), (0,)), ((), ())), precision=HIGHEST)
    cond_terms = jnp.broadcast_to(cond_terms[:, None], (count // s_n, s_n, short)).reshape(count, short)
    cond_total = lax.all_to_all(cond_terms, AXES, 0, 0, tiled=True).reshape(width)
    qkv_terms = settle(qkv_terms, F32, cond_total)
    _, silu_back = jax.vjp(jax.nn.silu, cond_own)
    cond_grad = silu_back(cond_total)[0].astype(BF16)[None]

    up_first = up_terms[:short].reshape(short, -1, 1, block_cols)
    up_second = up_terms[short:].reshape(short, -1, 1, block_cols)
    up_second = send(up_second, c=1)
    even = at["c"] == 0
    up_weight_grad = jnp.concatenate(
        [jnp.where(even, up_first, up_second), jnp.where(even, up_second, up_first)], axis=2
    ).reshape(short, hidden)
    qkv_terms = qkv_terms.reshape(groups, short, 3 * head_cols)
    arrived, table = [], []
    for c_d, s_d in np.ndindex(c_n, s_n):
        target = (at["c"] + c_d) % c_n * s_n + (at["s"] + s_d) % s_n
        part = lax.dynamic_index_in_dim(qkv_terms, target, 0, keepdims=False)
        arrived.append(send(part, c=c_d, s=s_d) if c_d + s_d else part)
        table.append((at["c"] - c_d) % c_n * s_n + (at["s"] - s_d) % s_n)
    qkv_weight_grad = place_columns(arrived, table, head_cols)
    return (
        block_out[None],
        input_grad[None],
        cond_grad,
        ada_weight_grad,
        ada_bias_grad,
        qkv_weight_grad,
        qv_bias_grad,
        out_weight_grad,
        out_bias_grad,
        up_weight_grad,
        up_bias_grad,
        down_weight_grad,
        down_bias_grad,
    )


def solution(mesh):
    tokens = P("batch", "seq", None)
    vector = P("batch", None)
    matrix, line = P(AXES, None), P(AXES)
    in_specs = (tokens, vector, tokens) + (matrix, line) * 5
    out_specs = (tokens, tokens, vector) + (matrix, line) * 5
    return jax.shard_map(
        partial(local, Grid(mesh)), mesh=mesh, in_specs=in_specs, out_specs=out_specs, check_vma=False
    )
```

```python
from functools import partial

import jax
import jax.numpy as jnp
import numpy as np
from jax import lax
from jax.experimental import pallas as pl
from jax.experimental.pallas import tpu as pltpu
from jax.sharding import PartitionSpec as P

HEAD_DIM = 64
SCALE = HEAD_DIM**-0.5
EPSILON = 1e-06
HIGHEST = lax.Precision.HIGHEST
F32, BF16 = jnp.float32, jnp.bfloat16
AXES = ("batch", "seq")
VMEM_LIMIT = 56 * 1024 * 1024
TILE = 256


def dot(left, right, dims, kind=F32):
    out = lax.dot_general(left, right, ((dims[:1], dims[1:]), ((), ())), preferred_element_type=F32)
    return out.astype(kind)


def after(value, *needed):
    return lax.optimization_barrier((value,) + needed)[0]


def settle(parts, kind, *needed):
    if needed:
        parts = lax.optimization_barrier(tuple(parts) + needed)[: len(parts)]
    return sum(part.astype(F32) for part in parts).astype(kind)


def normalize(values):
    average = jnp.mean(values, axis=-1, keepdims=True)
    centered = values - average
    variance = jnp.mean(centered * centered, axis=-1, keepdims=True)
    inverse = lax.rsqrt(variance + EPSILON)
    return centered * inverse, inverse


def normalize_back(grads, normed, inverse):
    average = jnp.mean(grads, axis=-1, keepdims=True)
    along = jnp.mean(grads * normed, axis=-1, keepdims=True)
    return inverse * (grads - average - normed * along)


class Grid:
    def __init__(self, mesh):
        batch, seq = mesh.shape["batch"], mesh.shape["seq"]
        self.size = {"z": batch // 4, "y": 2, "c": 2, "s": seq}
        self.shape = tuple(self.size.values())
        self.count = batch * seq

    def locate(self):
        batch, seq = lax.axis_index("batch"), lax.axis_index("seq")
        self.at = {"z": batch // 4, "y": (batch // 2) % 2, "c": batch % 2, "s": seq}
        self.me = batch * self.size["s"] + seq

    def send(self, value, **steps):
        moves = [steps.get(name, 0) for name in self.size]
        pairs = []
        for place in np.ndindex(*self.shape):
            target = tuple((p + m) % n for p, m, n in zip(place, moves, self.shape))
            pairs.append(
                (int(np.ravel_multi_index(place, self.shape)), int(np.ravel_multi_index(target, self.shape)))
            )
        return lax.ppermute(value, AXES, pairs)

    def steps(self, *names):
        return [dict(zip(names, at)) for at in np.ndindex(*[self.size[name] for name in names])]

    def arrivals(self, value, *names):
        return [self.send(value, **step) if any(step.values()) else value for step in self.steps(*names)]

    def gather(self, value, *names):
        return jnp.concatenate([part[None] for part in self.arrivals(value, *names)])

    def shed(self, terms, axis, name):
        n, me = self.size[name], self.at[name]
        parts = [lax.dynamic_index_in_dim(terms, (me + d) % n, axis, keepdims=False) for d in range(n)]
        self.sent = parts[1:]
        return [self.send(part, **{name: d}) if d else part for d, part in enumerate(parts)]

    def reduce(self, terms, axis, name, kind):
        return settle(self.shed(terms, axis, name), kind)

    def shard_of(self, back):
        index = 0
        for name, n in self.size.items():
            index = index * n + (self.at[name] - back.get(name, 0)) % n
        return index

    def sum_over(self, value, *names):
        return sum(self.arrivals(value, *names))


def place_kernel(jobs, flat, table, *refs):
    pieces, out, sems = refs[:-2], refs[-2], refs[-1]
    copies = []
    for at, (piece, block, unit, part) in enumerate(jobs):
        source = pieces[piece].at[block, unit]
        rows, columns = source.shape
        if flat:
            target = out.at[
                pl.ds(pl.multiple_of(table[at] * rows, rows), rows), pl.ds(part * columns, columns)
            ]
        else:
            target = out.at[table[at], part]
        copies.append(pltpu.make_async_copy(source, target, sems.at[at]))
        copies[-1].start()
    for copy in copies:
        copy.wait()


def place(pieces, jobs, table):
    rows, columns = pieces[0].shape[2:]
    parts = 1 + max(job[3] for job in jobs)
    count = len(jobs) // parts
    flat = rows % 16 == 0
    out = pl.pallas_call(
        partial(place_kernel, jobs, flat),
        out_shape=jax.ShapeDtypeStruct(
            (count * rows, parts * columns) if flat else (count, parts, rows, columns), pieces[0].dtype
        ),
        grid_spec=pltpu.PrefetchScalarGridSpec(
            num_scalar_prefetch=1,
            in_specs=[pl.BlockSpec(memory_space=pl.ANY)] * len(pieces),
            out_specs=pl.BlockSpec(memory_space=pltpu.VMEM if flat else pl.ANY),
            scratch_shapes=[pltpu.SemaphoreType.DMA((len(jobs),))],
        ),
        compiler_params=pltpu.CompilerParams(vmem_limit_bytes=VMEM_LIMIT),
        cost_estimate=pl.CostEstimate(
            flops=0, bytes_accessed=4 * len(jobs) * rows * columns, transcendentals=0
        ),
    )(jnp.stack(table).astype(jnp.int32), *pieces)
    if not flat:
        out = out.transpose(0, 2, 1, 3).reshape(count * rows, parts * columns)
    return out


def columns_kernel(width, table, *refs):
    pieces, out = refs[:-1], refs[-1]
    total = out.shape[1] // 3
    for at, piece in enumerate(pieces):
        for part in range(3):
            start = pl.multiple_of(part * total + table[at] * width, width)
            out[:, pl.ds(start, width)] = piece[:, part * width : (part + 1) * width]


def place_columns(pieces, table, width):
    rows, total = pieces[0].shape[0], len(pieces) * 3 * width
    if width % 128 != 0:
        out = jnp.zeros((rows, 3, total // 3), F32)
        for piece, group in zip(pieces, table):
            out = lax.dynamic_update_slice(out, piece.reshape(rows, 3, width), (0, 0, group * width))
        return out.reshape(rows, total)
    return pl.pallas_call(
        partial(columns_kernel, width),
        out_shape=jax.ShapeDtypeStruct((rows, total), F32),
        grid_spec=pltpu.PrefetchScalarGridSpec(
            num_scalar_prefetch=1,
            in_specs=[pl.BlockSpec(memory_space=pltpu.VMEM)] * len(pieces),
            out_specs=pl.BlockSpec(memory_space=pltpu.VMEM),
        ),
    )(jnp.stack(table).astype(jnp.int32), *pieces)


def head_mask(width, head):
    lanes = lax.broadcasted_iota(jnp.int32, (1, width), 1)
    return (lanes >= head * HEAD_DIM) & (lanes < (head + 1) * HEAD_DIM)


def attend_kernel(width, qkv, out, logsum):
    tokens = qkv.shape[1]
    step = min(128, width)
    tile = min(TILE, tokens)
    for start in range(0, width, step):
        keys = qkv[0, :, width + start : width + start + step]
        values = qkv[0, :, 2 * width + start : 2 * width + start + step]
        for row in range(0, tokens, tile):
            queries = qkv[0, row : row + tile, start : start + step] * jnp.asarray(SCALE, BF16)
            total, sums = None, None
            for head in range(step // HEAD_DIM):
                mask = head_mask(step, head)
                scores = dot(jnp.where(mask, queries, jnp.zeros_like(queries)), keys, (1, 1))
                top = jnp.max(scores, axis=1, keepdims=True)
                powers = jnp.exp(scores - top)
                weight = jnp.sum(powers, axis=1, keepdims=True)
                part = dot(powers.astype(BF16), values, (1, 0)) / weight
                level = jnp.broadcast_to(top + jnp.log(weight), part.shape)
                total = part if total is None else jnp.where(mask, part, total)
                sums = level if sums is None else jnp.where(mask, level, sums)
            out[0, row : row + tile, start : start + step] = total.astype(BF16)
            logsum[0, row : row + tile, start : start + step] = sums


def attend(qkv, latent, width):
    _, tokens, _ = qkv.shape
    spec = lambda columns, at: pl.BlockSpec((1, tokens, columns), lambda l: (at, 0, 0))
    return pl.pallas_call(
        partial(attend_kernel, width),
        grid=(1,),
        in_specs=[spec(3 * width, latent)],
        out_specs=[spec(width, 0), spec(width, 0)],
        out_shape=[
            jax.ShapeDtypeStruct((1, tokens, width), BF16),
            jax.ShapeDtypeStruct((1, tokens, width), F32),
        ],
        compiler_params=pltpu.CompilerParams(vmem_limit_bytes=VMEM_LIMIT),
        cost_estimate=pl.CostEstimate(
            flops=tokens * tokens * width,
            bytes_accessed=12 * tokens * width,
            transcendentals=0,
        ),
    )(qkv)


def attend_back_kernel(width, qkv, grads, logsum, out, key_sum, value_sum):
    tokens = qkv.shape[1]
    step = min(128, width)
    tile = min(TILE, tokens)
    for start in range(0, width, step):
        keys = qkv[0, :, width + start : width + start + step]
        values = qkv[0, :, 2 * width + start : 2 * width + start + step]
        key_sum[...] = jnp.zeros_like(key_sum)
        value_sum[...] = jnp.zeros_like(value_sum)
        for row in range(0, tokens, tile):
            queries = qkv[0, row : row + tile, start : start + step] * jnp.asarray(SCALE, BF16)
            grad = grads[0, row : row + tile, start : start + step]
            query_grad = None
            for head in range(step // HEAD_DIM):
                mask = head_mask(step, head)
                own_queries = jnp.where(mask, queries, jnp.zeros_like(queries))
                own_grad = jnp.where(mask, grad, jnp.zeros_like(grad))
                lane = start + head * HEAD_DIM
                level = logsum[0, row : row + tile, lane : lane + 1]
                probs = jnp.exp(dot(own_queries, keys, (1, 1)) - level)
                prob_grad = dot(own_grad, values, (1, 1))
                inner = jnp.sum(probs * prob_grad, axis=1, keepdims=True)
                score_grad = (probs * (prob_grad - inner)).astype(BF16)
                part = dot(score_grad, keys, (1, 0))
                query_grad = part if query_grad is None else jnp.where(mask, part, query_grad)
                key_sum[...] += dot(score_grad, own_queries, (0, 0))
                value_sum[...] += dot(probs.astype(BF16), own_grad, (0, 0))
            out[0, row : row + tile, start : start + step] = (query_grad * SCALE).astype(BF16)
        out[0, :, width + start : width + start + step] = key_sum[...].astype(BF16)
        out[0, :, 2 * width + start : 2 * width + start + step] = value_sum[...].astype(BF16)


def attend_back(qkv, grads, logsum, latent, width):
    _, tokens, _ = qkv.shape
    step = min(128, width)
    spec = lambda columns, at: pl.BlockSpec((1, tokens, columns), lambda l: (at, 0, 0))
    return pl.pallas_call(
        partial(attend_back_kernel, width),
        grid=(1,),
        in_specs=[spec(3 * width, latent), spec(width, 0), spec(width, 0)],
        out_specs=spec(3 * width, 0),
        out_shape=jax.ShapeDtypeStruct((1, tokens, 3 * width), BF16),
        scratch_shapes=[pltpu.VMEM((tokens, step), F32), pltpu.VMEM((tokens, step), F32)],
        compiler_params=pltpu.CompilerParams(vmem_limit_bytes=VMEM_LIMIT),
        cost_estimate=pl.CostEstimate(
            flops=2 * tokens * tokens * width,
            bytes_accessed=18 * tokens * width,
            transcendentals=0,
        ),
    )(qkv, grads, logsum)


def local(
    grid,
    block_in,
    conditioning,
    cotangent,
    ada_weight,
    ada_bias,
    qkv_weight,
    qv_bias,
    out_weight,
    out_bias,
    up_weight,
    up_bias,
    down_weight,
    down_bias,
):
    grid.locate()
    size, at = grid.size, grid.at
    z_n, y_n, c_n, s_n = grid.shape
    _, rows, width = block_in.shape
    hidden = up_weight.shape[1]
    count = grid.count
    groups = c_n * s_n
    head_cols = width // groups
    short = width // count
    long = hidden // count
    block_cols = s_n * long
    half = hidden // 2
    own_group = at["c"] * s_n + at["s"]
    send = grid.send

    cond_own = conditioning[0].astype(F32)
    cond_act = jax.nn.silu(cond_own).astype(BF16)
    shares = jnp.concatenate([qv_bias, out_bias, up_bias, down_bias, cond_act])
    cols = qkv_weight.reshape(short, 3, groups, head_cols)
    blocks = []
    for c_d, s_d in np.ndindex(c_n, s_n):
        target = (at["c"] + c_d) % c_n * s_n + (at["s"] + s_d) % s_n
        part = lax.dynamic_index_in_dim(cols, target, 2, keepdims=False).reshape(short, 3 * head_cols)
        blocks.append(send(part, c=c_d, s=s_d) if c_d + s_d else part)
    x_own = block_in[0]
    shares = after(jnp.broadcast_to(shares[None], (count,) + shares.shape), *blocks)
    qkv_z = grid.gather(jnp.concatenate([block[None] for block in blocks]), "z")
    all_shares = lax.all_to_all(shares, AXES, 0, 0, tiled=True)
    x_all = grid.gather(x_own, "s")
    all_shares = after(all_shares, x_all)
    cuts = np.cumsum([qv_bias.shape[0], out_bias.shape[0], up_bias.shape[0]])
    bias_cols = shares.shape[1] - width
    b_qv, b_out, b_up, b_down = [
        part.reshape(-1).astype(F32) for part in jnp.split(all_shares[:, :bias_cols], cuts, axis=1)
    ]

    cond_all = all_shares[:, bias_cols:].reshape(count // s_n, s_n, width)[:, 0]
    cond_flat = lax.dynamic_slice_in_dim(cond_all, grid.me * short, short, axis=1)
    bias_row = lax.dynamic_update_slice(
        jnp.zeros((6 * width,), F32), ada_bias.astype(F32), (grid.me * ada_bias.shape[0],)
    )
    terms = (dot(cond_flat, ada_weight, (1, 0)) + bias_row).reshape(count, 6 * width // s_n)
    terms = lax.all_to_all(after(terms, qkv_z), AXES, 0, 0, tiled=True)
    small_z = terms
    parts = grid.arrivals(after(qkv_z, terms), "y")
    terms = grid.gather(jnp.sum(terms, axis=0), "s")
    modulation = jnp.concatenate(
        [lax.dynamic_index_in_dim(terms, (at["s"] - s) % s_n, 0, keepdims=False) for s in range(s_n)]
    )
    shift_attn, scale_attn, gate_attn, shift_mlp, scale_mlp, gate_mlp = jnp.split(modulation, 6)

    jobs, table = [], []
    for i, back in enumerate(grid.steps("y", "z")):
        piece, block = divmod(i, z_n)
        for group, (c_d, s_d) in enumerate(np.ndindex(c_n, s_n)):
            jobs.append((piece, block * groups + group, 0, 0))
            table.append(grid.shard_of({**back, "c": c_d, "s": s_d}))
    w_qkv = place([part.reshape(-1, 1, short, 3 * head_cols) for part in parts], jobs, table)

    wide = half // width
    up_cols = up_weight.reshape(short, z_n * y_n, c_n, block_cols)
    up_own = lax.dynamic_index_in_dim(up_cols, at["c"], 2, keepdims=False).reshape(short, wide, width)
    up_other = lax.dynamic_index_in_dim(up_cols, 1 - at["c"], 2, keepdims=False).reshape(short, wide, width)
    up_other = send(after(up_other, x_all), c=1)
    units = [out_weight] + [rows_of[:, i] for rows_of in (up_own, up_other) for i in range(wide)]
    units = jnp.concatenate([unit[None] for unit in units])
    orders = (("s", "y"), ("y", "s"))
    units_z = grid.arrivals(after(units, small_z), "z")
    up_first = [
        grid.arrivals(jnp.concatenate([part[None, low:high] for part in units_z]), order[0])
        for low, high, order in ((0, 1 + wide, orders[0]), (1 + wide, 1 + 2 * wide, orders[1]))
    ]
    inputs = x_own.astype(F32)
    normed_all, inverse_all = normalize(x_all.astype(F32))
    modded_all = (normed_all * (1.0 + scale_attn) + shift_attn).astype(BF16).reshape(s_n * rows, width)
    modded_all = jnp.concatenate([modded_all, send(modded_all, c=1)])
    q_bias = lax.dynamic_index_in_dim(b_qv[:width].reshape(groups, head_cols), own_group, 0, keepdims=False)
    v_bias = lax.dynamic_index_in_dim(b_qv[width:].reshape(groups, head_cols), own_group, 0, keepdims=False)
    qkv_bias = jnp.concatenate([q_bias, jnp.zeros_like(q_bias), v_bias])
    qkv = (dot(modded_all, w_qkv, (1, 0)) + qkv_bias).astype(BF16).reshape(c_n, s_n * rows, 3 * head_cols)
    up_first = [jnp.concatenate([after(part, qkv)[None] for part in parts]) for parts in up_first]
    down_z = grid.arrivals(after(down_weight.reshape(2, long // 2, width), *up_first), "z")
    up_last = [grid.arrivals(after(part, *up_first), order[1]) for part, order in zip(up_first, orders)]
    down_first = [
        grid.gather(jnp.concatenate([part[None, i : i + 1] for part in down_z]), order[0])
        for i, order in enumerate(orders)
    ]
    attended_all, logsums = [], []
    for latent in range(c_n):
        qkv = after(qkv, *(attended_all + down_z if latent else up_first))
        part, logsum = attend(qkv, latent, head_cols)
        attended_all.append(part.reshape(s_n, rows, head_cols))
        logsums.append(logsum)
    arrived = []
    for c_d, s_d in np.ndindex(c_n, s_n):
        part = attended_all[c_d][s_d]
        if c_d + s_d:
            part = after(part, *attended_all)
        arrived.append(send(part, c=-c_d, s=-s_d) if c_d + s_d else part)
    up_steps = [grid.steps(order[1], order[0], "z") for order in orders]
    each = count // (c_n * grid.size["y"])
    flat_last = lax.optimization_barrier(tuple(part for parts in up_last for part in parts) + tuple(attended_all))
    parts = [part.reshape((-1,) + part.shape[2:]) for part in flat_last[: -len(attended_all)]]
    jobs, table, out_jobs, out_table = [], [], [], []
    first = 0
    for c_d, (last, steps) in enumerate(zip(up_last, up_steps)):
        per = len(steps) // len(last)
        for i, back in enumerate(steps):
            piece, block = divmod(i, per)
            for part in range(wide):
                jobs.append((first + piece, block, part + 1 - c_d, part))
                table.append(grid.shard_of({**back, "c": c_d}))
        first += len(last)
    out_own = jnp.concatenate([part[:, :1] for part in parts[: len(up_last[0])]])
    for c_d in range(c_n):
        for i, back in enumerate(up_steps[0]):
            out_jobs.append((c_d, i, 0, 0))
            out_table.append(grid.shard_of({**back, "c": c_d}))
    w_out = place([out_own, send(out_own, c=1)], out_jobs, out_table)
    w_up = place(parts, jobs, table)
    stacked = jnp.stack(arrived)
    ordered = []
    for c in range(c_n):
        for s in range(s_n):
            index = (c - at["c"]) % c_n * s_n + (s - at["s"]) % s_n
            ordered.append(lax.dynamic_index_in_dim(stacked, index, 0, keepdims=False))
    attended = jnp.concatenate(ordered, axis=1)
    down_last = [grid.arrivals(after(part, *arrived), order[1]) for part, order in zip(down_first, orders)]
    attn_proj = dot(after(attended, w_up), w_out, (1, 0)) + b_out
    attn_proj = after(attn_proj, *down_first)
    middle = inputs + gate_attn * attn_proj
    normed_mid, inverse_mid = normalize(middle)
    modded_mlp = (normed_mid * (1.0 + scale_mlp) + shift_mlp).astype(BF16)
    mlp_all = jnp.concatenate([modded_mlp, send(modded_mlp, c=1)])
    up_half = lax.dynamic_index_in_dim(b_up.reshape(-1, c_n, block_cols), at["c"], 1, keepdims=False).reshape(half)
    pre_act = dot(mlp_all, w_up, (1, 0)) + up_half
    gelu_tanh = partial(jax.nn.gelu, approximate=True)
    activated = gelu_tanh(pre_act).astype(BF16)
    out_cot = cotangent[0].astype(F32)
    mlp_grad = (gate_mlp * out_cot).astype(BF16)
    mlp_grad_all = jnp.concatenate([mlp_grad, send(mlp_grad, c=1)])
    down_terms = dot(activated, mlp_grad_all, (0, 0), BF16).reshape(z_n, y_n, s_n, long, width)
    flat_last = lax.optimization_barrier((down_terms,) + tuple(part for parts in down_last for part in parts))
    down_terms = flat_last[0]
    down_a = grid.shed(down_terms[..., : long // 2, :], 2, "s")
    down_sent = grid.sent
    down_b = grid.shed(down_terms[..., long // 2 :, :], 1, "y")
    down_sent = down_sent + grid.sent
    parts = [part.reshape((-1,) + part.shape[2:]) for part in flat_last[1:]]
    jobs, table = [], []
    first = 0
    for row_half, (last, order) in enumerate(zip(down_last, orders)):
        steps = grid.steps(order[1], order[0], "z")
        per = len(steps) // len(last)
        for i, back in enumerate(steps):
            shard = grid.shard_of(back)
            piece, block = divmod(i, per)
            jobs.append((first + piece, block, 0, 0))
            table.append((shard // (c_n * s_n) * s_n + shard % s_n) * 2 + row_half)
        first += len(last)
    w_down = place(parts, jobs, table)
    proj_terms = dot(after(activated, *down_sent), w_down, (1, 0))
    mlp_proj = proj_terms[:rows] + send(proj_terms[rows:], c=1) + b_down
    block_out = (middle + gate_mlp * mlp_proj).astype(BF16)

    down_bias_grad = jnp.sum(mlp_grad.astype(F32), axis=0)
    act_grad = dot(after(mlp_grad_all, proj_terms, *down_sent), w_down, (1, 1))
    _, gelu_back = jax.vjp(gelu_tanh, pre_act)
    pre_grad = gelu_back(act_grad)[0].astype(BF16)
    up_bias_grad = jnp.sum(pre_grad.astype(F32), axis=0)
    down_a, down_b = settle(down_a, BF16, pre_grad), settle(down_b, BF16, pre_grad)
    up_terms = dot(after(mlp_all, down_a, down_b), pre_grad, (0, 0), BF16)
    up_terms = up_terms.reshape(z_n, y_n, c_n, s_n, short, half)
    up_a = grid.shed(lax.dynamic_index_in_dim(up_terms, at["c"], 2, keepdims=False), 1, "y")
    up_sent = grid.sent
    up_b = grid.shed(lax.dynamic_index_in_dim(up_terms, 1 - at["c"], 2, keepdims=False), 2, "s")
    up_sent = up_sent + grid.sent
    down_a, down_b = grid.shed(down_a, 1, "y"), grid.shed(down_b, 1, "s")
    mod_terms = dot(after(pre_grad, *up_sent), w_up, (1, 1))
    arrived = send(mod_terms[rows:].astype(BF16), c=1)
    up_a, up_b = settle(up_a, BF16, mod_terms, arrived), settle(up_b, BF16, mod_terms, arrived)
    mlp_mod_grad = after(mod_terms[:rows], up_a, up_b) + arrived.astype(F32)
    middle_part = normalize_back(mlp_mod_grad * (1.0 + scale_mlp), normed_mid, inverse_mid)
    shift_mlp_grad = jnp.sum(mlp_mod_grad, axis=0)
    scale_mlp_grad = jnp.sum(mlp_mod_grad * normed_mid, axis=0)
    middle_grad = out_cot + middle_part
    gate_mlp_grad = jnp.sum(out_cot * mlp_proj, axis=0)
    attn_grad = (gate_attn * middle_grad).astype(BF16)
    down_terms = jnp.concatenate([settle(part, BF16, attn_grad) for part in (down_a, down_b)], axis=1)
    attn_grad = after(attn_grad, down_terms)
    gate_attn_grad = jnp.sum(middle_grad * attn_proj, axis=0)
    out_bias_grad = jnp.sum(attn_grad.astype(F32), axis=0)
    attended_grad = dot(attn_grad, w_out, (1, 1), BF16)
    arrived = []
    for c_d in range(c_n):
        for s_d in range(s_n):
            target = (at["c"] + c_d) % c_n * s_n + (at["s"] + s_d) % s_n
            part = lax.dynamic_slice_in_dim(attended_grad, target * head_cols, head_cols, axis=1)
            arrived.append(send(part, c=c_d, s=s_d) if c_d + s_d else part)
    up_a, up_b = after(up_a, *arrived), after(up_b, *arrived)
    up_a, up_b = grid.shed(up_a, 1, "s"), grid.shed(up_b, 1, "y")
    down_terms = grid.shed(down_terms, 0, "z")
    out_terms = dot(attended, after(attn_grad, attended_grad), (0, 0), BF16)
    out_terms = out_terms.reshape(z_n, y_n, c_n, s_n, short, width)
    out_terms = grid.reduce(out_terms, 2, "c", BF16)
    out_terms = grid.shed(out_terms, 2, "s")
    out_sent = grid.sent
    qkv_grads = []
    for latent in range(c_n):
        grads = jnp.concatenate(arrived[latent * s_n : (latent + 1) * s_n])[None]
        if latent == 0:
            grads = after(grads, *out_sent)
        else:
            down_weight_grad = settle(down_terms, F32, *qkv_grads)
            up_terms = jnp.concatenate([settle(part, BF16, *qkv_grads) for part in (up_a, up_b)], axis=1)
            up_terms = grid.shed(up_terms, 0, "z")
            grads = after(grads, down_weight_grad, *grid.sent)
        qkv_grads.append(attend_back(qkv, grads, logsums[latent], latent, head_cols))
    qkv_grad = jnp.concatenate(qkv_grads).reshape(c_n * s_n * rows, 3 * head_cols)
    up_terms = settle(up_terms, F32, qkv_grad)
    out_terms = grid.shed(settle(out_terms, BF16, qkv_grad), 1, "y")
    qkv_grad = after(qkv_grad, up_terms, *grid.sent)
    mod_terms = dot(qkv_grad, w_qkv, (1, 1)).reshape(c_n, s_n, rows, width)
    mod_sent = mod_terms[1].astype(BF16)
    qkv_terms = dot(modded_all, after(qkv_grad, mod_sent), (0, 0), BF16)
    qkv_terms = qkv_terms.reshape(z_n, y_n, c_n, s_n, short, 3 * head_cols)
    qkv_terms = grid.shed(qkv_terms, 1, "y")
    out_terms = settle(out_terms, BF16, *grid.sent)
    mod_terms = after(mod_terms[0], *grid.sent)
    mod_sum = mod_terms + send(mod_sent, c=1).astype(F32)
    shift_attn_grad = jnp.sum(mod_sum, axis=(0, 1))
    scale_attn_grad = jnp.sum(mod_sum * normed_all, axis=(0, 1))
    column_sums = jnp.sum(qkv_grad.astype(F32), axis=0)
    arrived = [send(mod_sum[d].astype(BF16), s=-d) for d in range(1, s_n)]

    modulation_grad = jnp.concatenate(
        [shift_attn_grad, scale_attn_grad, gate_attn_grad, shift_mlp_grad, scale_mlp_grad, gate_mlp_grad]
    )
    def spread(value, index, n, axis):
        shape = value.shape[:axis] + (n,) + value.shape[axis:]
        start = tuple(index if i == axis else 0 for i in range(len(shape)))
        return lax.dynamic_update_slice(jnp.zeros(shape, F32), jnp.expand_dims(value, axis), start)

    q_sums = spread(column_sums[:head_cols], own_group, groups, 0).reshape(-1)
    v_sums = spread(column_sums[2 * head_cols :], own_group, groups, 0).reshape(-1)
    up_sums = spread(up_bias_grad.reshape(-1, block_cols), at["c"], c_n, 1).reshape(-1)
    total = jnp.concatenate([modulation_grad, q_sums, v_sums, out_bias_grad, up_sums, down_bias_grad])
    total = grid.sum_over(total, "s")
    qkv_terms = lax.optimization_barrier(tuple(qkv_terms) + (total,))
    qkv_terms, total = qkv_terms[:-1], qkv_terms[-1]
    total = grid.gather(total, "z")
    qkv_terms = settle(qkv_terms, BF16, total)
    total = grid.gather(total, "c", "y")
    qkv_terms = grid.shed(after(qkv_terms, total), 0, "z")
    out_terms = grid.shed(after(out_terms, *grid.sent), 0, "z")
    total = after(total, *grid.sent)
    attn_mod_grad = mod_sum[0]
    for part in arrived:
        part = after(part, total)
        attn_mod_grad = attn_mod_grad + part.astype(F32)
    input_part = normalize_back(attn_mod_grad * (1.0 + scale_attn), normed_all[0], inverse_all[0])
    input_grad = (middle_grad + input_part).astype(BF16)
    z, y, c = ((at[name] - jnp.arange(size[name])) % size[name] for name in ("z", "y", "c"))
    latent = ((z[None, None] * y_n + y[None, :, None]) * c_n + c[:, None, None]).reshape(-1)
    cond_back = jnp.dot(jax.nn.one_hot(latent, count // s_n, dtype=BF16), cond_flat, preferred_element_type=F32)
    mod_grads = total.reshape(-1, total.shape[-1])[:, : 6 * width]
    bias_sums = jnp.sum(total.reshape(-1, total.shape[-1]), axis=0)

    def own_share(start, kept):
        return lax.dynamic_slice_in_dim(bias_sums[start : start + kept * count], grid.me * kept, kept)

    ada_bias_grad = own_share(0, ada_bias.shape[0])
    start = 6 * width
    bias_grads = []
    for bias in (qv_bias, out_bias, up_bias, down_bias):
        bias_grads.append(own_share(start, bias.shape[0]))
        start += bias.shape[0] * count
    qv_bias_grad, out_bias_grad, up_bias_grad, down_bias_grad = bias_grads
    ada_weight_grad = lax.dot_general(
        cond_back, mod_grads, (((0,), (0,)), ((), ())), precision=HIGHEST
    )
    cond_terms = lax.dot_general(
        mod_grads, ada_weight.astype(F32), (((1,), (1,)), ((), ())), precision=HIGHEST
    )
    order = (latent[:, None] == jnp.arange(count // s_n)[None]).astype(F32)
    cond_terms = lax.dot_general(order, cond_terms, (((0,), (0,)), ((), ())), precision=HIGHEST)
    cond_terms = jnp.broadcast_to(cond_terms[:, None], (count // s_n, s_n, short)).reshape(count, short)
    cond_terms = after(cond_terms, part)
    cond_total = lax.all_to_all(cond_terms, AXES, 0, 0, tiled=True).reshape(width)
    cond_total = after(cond_total, input_grad)
    qkv_terms = settle(qkv_terms, F32, cond_total)
    out_weight_grad = settle(out_terms, F32, cond_total)
    _, silu_back = jax.vjp(jax.nn.silu, cond_own)
    cond_grad = silu_back(cond_total)[0].astype(BF16)[None]

    up_terms = after(up_terms, total)
    up_first = up_terms[:short].reshape(short, -1, 1, block_cols)
    up_second = up_terms[short:].reshape(short, -1, 1, block_cols)
    up_second = send(up_second, c=1)
    even = at["c"] == 0
    up_weight_grad = jnp.concatenate(
        [jnp.where(even, up_first, up_second), jnp.where(even, up_second, up_first)], axis=2
    ).reshape(short, hidden)
    qkv_terms = qkv_terms.reshape(groups, short, 3 * head_cols)
    arrived, table = [], []
    for c_d, s_d in np.ndindex(c_n, s_n):
        target = (at["c"] + c_d) % c_n * s_n + (at["s"] + s_d) % s_n
        part = lax.dynamic_index_in_dim(qkv_terms, target, 0, keepdims=False)
        arrived.append(send(part, c=c_d, s=s_d) if c_d + s_d else part)
        table.append((at["c"] - c_d) % c_n * s_n + (at["s"] - s_d) % s_n)
    qkv_weight_grad = place_columns(arrived, table, head_cols)
    return (
        block_out[None],
        input_grad[None],
        cond_grad,
        ada_weight_grad,
        ada_bias_grad,
        qkv_weight_grad,
        qv_bias_grad,
        out_weight_grad,
        out_bias_grad,
        up_weight_grad,
        up_bias_grad,
        down_weight_grad,
        down_bias_grad,
    )


def solution(mesh):
    tokens = P("batch", "seq", None)
    vector = P("batch", None)
    matrix, line = P(AXES, None), P(AXES)
    in_specs = (tokens, vector, tokens) + (matrix, line) * 5
    out_specs = (tokens, tokens, vector) + (matrix, line) * 5
    return jax.shard_map(
        partial(local, Grid(mesh)), mesh=mesh, in_specs=in_specs, out_specs=out_specs, check_vma=False
    )
```

```python
from functools import partial

import jax
import jax.numpy as jnp
import numpy as np
from jax import lax
from jax.experimental import pallas as pl
from jax.experimental.pallas import tpu as pltpu
from jax.sharding import PartitionSpec as P

HEAD_DIM = 64
SCALE = HEAD_DIM**-0.5
EPSILON = 1e-06
HIGHEST = lax.Precision.HIGHEST
F32, BF16 = jnp.float32, jnp.bfloat16
AXES = ("batch", "seq")
VMEM_LIMIT = 56 * 1024 * 1024
TILE = 256


def dot(left, right, dims, kind=F32):
    out = lax.dot_general(left, right, ((dims[:1], dims[1:]), ((), ())), preferred_element_type=F32)
    return out.astype(kind)


def after(value, *needed):
    return lax.optimization_barrier((value,) + needed)[0]


def settle(parts, kind, *needed):
    if needed:
        parts = lax.optimization_barrier(tuple(parts) + needed)[: len(parts)]
    return sum(part.astype(F32) for part in parts).astype(kind)


def normalize(values):
    average = jnp.mean(values, axis=-1, keepdims=True)
    centered = values - average
    variance = jnp.mean(centered * centered, axis=-1, keepdims=True)
    inverse = lax.rsqrt(variance + EPSILON)
    return centered * inverse, inverse


def normalize_back(grads, normed, inverse):
    average = jnp.mean(grads, axis=-1, keepdims=True)
    along = jnp.mean(grads * normed, axis=-1, keepdims=True)
    return inverse * (grads - average - normed * along)


class Grid:
    def __init__(self, mesh):
        batch, seq = mesh.shape["batch"], mesh.shape["seq"]
        self.size = {"z": batch // 4, "y": 2, "c": 2, "s": seq}
        self.shape = tuple(self.size.values())
        self.count = batch * seq

    def locate(self):
        batch, seq = lax.axis_index("batch"), lax.axis_index("seq")
        self.at = {"z": batch // 4, "y": (batch // 2) % 2, "c": batch % 2, "s": seq}
        self.me = batch * self.size["s"] + seq

    def send(self, value, **steps):
        moves = [steps.get(name, 0) for name in self.size]
        pairs = []
        for place in np.ndindex(*self.shape):
            target = tuple((p + m) % n for p, m, n in zip(place, moves, self.shape))
            pairs.append(
                (int(np.ravel_multi_index(place, self.shape)), int(np.ravel_multi_index(target, self.shape)))
            )
        return lax.ppermute(value, AXES, pairs)

    def steps(self, *names):
        return [dict(zip(names, at)) for at in np.ndindex(*[self.size[name] for name in names])]

    def arrivals(self, value, *names):
        return [self.send(value, **step) if any(step.values()) else value for step in self.steps(*names)]

    def gather(self, value, *names):
        return jnp.concatenate([part[None] for part in self.arrivals(value, *names)])

    def shed(self, terms, axis, name):
        n, me = self.size[name], self.at[name]
        parts = [lax.dynamic_index_in_dim(terms, (me + d) % n, axis, keepdims=False) for d in range(n)]
        self.sent = parts[1:]
        return [self.send(part, **{name: d}) if d else part for d, part in enumerate(parts)]

    def reduce(self, terms, axis, name, kind):
        return settle(self.shed(terms, axis, name), kind)

    def shard_of(self, back):
        index = 0
        for name, n in self.size.items():
            index = index * n + (self.at[name] - back.get(name, 0)) % n
        return index

    def sum_over(self, value, *names):
        return sum(self.arrivals(value, *names))


def place_kernel(jobs, flat, table, *refs):
    pieces, out, sems = refs[:-2], refs[-2], refs[-1]
    copies = []
    for at, (piece, block, unit, part) in enumerate(jobs):
        source = pieces[piece].at[block, unit]
        rows, columns = source.shape
        if flat:
            target = out.at[
                pl.ds(pl.multiple_of(table[at] * rows, rows), rows), pl.ds(part * columns, columns)
            ]
        else:
            target = out.at[table[at], part]
        copies.append(pltpu.make_async_copy(source, target, sems.at[at]))
        copies[-1].start()
    for copy in copies:
        copy.wait()


def place(pieces, jobs, table):
    rows, columns = pieces[0].shape[2:]
    parts = 1 + max(job[3] for job in jobs)
    count = len(jobs) // parts
    flat = rows % 16 == 0
    out = pl.pallas_call(
        partial(place_kernel, jobs, flat),
        out_shape=jax.ShapeDtypeStruct(
            (count * rows, parts * columns) if flat else (count, parts, rows, columns), pieces[0].dtype
        ),
        grid_spec=pltpu.PrefetchScalarGridSpec(
            num_scalar_prefetch=1,
            in_specs=[pl.BlockSpec(memory_space=pl.ANY)] * len(pieces),
            out_specs=pl.BlockSpec(memory_space=pltpu.VMEM if flat else pl.ANY),
            scratch_shapes=[pltpu.SemaphoreType.DMA((len(jobs),))],
        ),
        compiler_params=pltpu.CompilerParams(vmem_limit_bytes=VMEM_LIMIT),
        cost_estimate=pl.CostEstimate(
            flops=0, bytes_accessed=4 * len(jobs) * rows * columns, transcendentals=0
        ),
    )(jnp.stack(table).astype(jnp.int32), *pieces)
    if not flat:
        out = out.transpose(0, 2, 1, 3).reshape(count * rows, parts * columns)
    return out


def columns_kernel(width, table, *refs):
    pieces, out = refs[:-1], refs[-1]
    total = out.shape[1] // 3
    for at, piece in enumerate(pieces):
        for part in range(3):
            start = pl.multiple_of(part * total + table[at] * width, width)
            out[:, pl.ds(start, width)] = piece[:, part * width : (part + 1) * width]


def place_columns(pieces, table, width):
    rows, total = pieces[0].shape[0], len(pieces) * 3 * width
    if width % 128 != 0:
        out = jnp.zeros((rows, 3, total // 3), F32)
        for piece, group in zip(pieces, table):
            out = lax.dynamic_update_slice(out, piece.reshape(rows, 3, width), (0, 0, group * width))
        return out.reshape(rows, total)
    return pl.pallas_call(
        partial(columns_kernel, width),
        out_shape=jax.ShapeDtypeStruct((rows, total), F32),
        grid_spec=pltpu.PrefetchScalarGridSpec(
            num_scalar_prefetch=1,
            in_specs=[pl.BlockSpec(memory_space=pltpu.VMEM)] * len(pieces),
            out_specs=pl.BlockSpec(memory_space=pltpu.VMEM),
        ),
    )(jnp.stack(table).astype(jnp.int32), *pieces)


def head_mask(width, head):
    lanes = lax.broadcasted_iota(jnp.int32, (1, width), 1)
    return (lanes >= head * HEAD_DIM) & (lanes < (head + 1) * HEAD_DIM)


def attend_kernel(width, qkv, out, logsum):
    tokens = qkv.shape[1]
    step = min(128, width)
    tile = min(TILE, tokens)
    for start in range(0, width, step):
        keys = qkv[0, :, width + start : width + start + step]
        values = qkv[0, :, 2 * width + start : 2 * width + start + step]
        for row in range(0, tokens, tile):
            queries = qkv[0, row : row + tile, start : start + step] * jnp.asarray(SCALE, BF16)
            total, sums = None, None
            for head in range(step // HEAD_DIM):
                mask = head_mask(step, head)
                scores = dot(jnp.where(mask, queries, jnp.zeros_like(queries)), keys, (1, 1))
                top = jnp.max(scores, axis=1, keepdims=True)
                powers = jnp.exp(scores - top)
                weight = jnp.sum(powers, axis=1, keepdims=True)
                part = dot(powers.astype(BF16), values, (1, 0)) / weight
                level = jnp.broadcast_to(top + jnp.log(weight), part.shape)
                total = part if total is None else jnp.where(mask, part, total)
                sums = level if sums is None else jnp.where(mask, level, sums)
            out[0, row : row + tile, start : start + step] = total.astype(BF16)
            logsum[0, row : row + tile, start : start + step] = sums


def attend(qkv, latent, width):
    _, tokens, _ = qkv.shape
    spec = lambda columns, at: pl.BlockSpec((1, tokens, columns), lambda l: (at, 0, 0))
    return pl.pallas_call(
        partial(attend_kernel, width),
        grid=(1,),
        in_specs=[spec(3 * width, latent)],
        out_specs=[spec(width, 0), spec(width, 0)],
        out_shape=[
            jax.ShapeDtypeStruct((1, tokens, width), BF16),
            jax.ShapeDtypeStruct((1, tokens, width), F32),
        ],
        compiler_params=pltpu.CompilerParams(vmem_limit_bytes=VMEM_LIMIT),
        cost_estimate=pl.CostEstimate(
            flops=tokens * tokens * width,
            bytes_accessed=12 * tokens * width,
            transcendentals=0,
        ),
    )(qkv)


def attend_back_kernel(width, qkv, grads, logsum, out, key_sum, value_sum):
    tokens = qkv.shape[1]
    step = min(128, width)
    tile = min(TILE, tokens)
    for start in range(0, width, step):
        keys = qkv[0, :, width + start : width + start + step]
        values = qkv[0, :, 2 * width + start : 2 * width + start + step]
        key_sum[...] = jnp.zeros_like(key_sum)
        value_sum[...] = jnp.zeros_like(value_sum)
        for row in range(0, tokens, tile):
            queries = qkv[0, row : row + tile, start : start + step] * jnp.asarray(SCALE, BF16)
            grad = grads[0, row : row + tile, start : start + step]
            query_grad = None
            for head in range(step // HEAD_DIM):
                mask = head_mask(step, head)
                own_queries = jnp.where(mask, queries, jnp.zeros_like(queries))
                own_grad = jnp.where(mask, grad, jnp.zeros_like(grad))
                lane = start + head * HEAD_DIM
                level = logsum[0, row : row + tile, lane : lane + 1]
                probs = jnp.exp(dot(own_queries, keys, (1, 1)) - level)
                prob_grad = dot(own_grad, values, (1, 1))
                inner = jnp.sum(probs * prob_grad, axis=1, keepdims=True)
                score_grad = (probs * (prob_grad - inner)).astype(BF16)
                part = dot(score_grad, keys, (1, 0))
                query_grad = part if query_grad is None else jnp.where(mask, part, query_grad)
                key_sum[...] += dot(score_grad, own_queries, (0, 0))
                value_sum[...] += dot(probs.astype(BF16), own_grad, (0, 0))
            out[0, row : row + tile, start : start + step] = (query_grad * SCALE).astype(BF16)
        out[0, :, width + start : width + start + step] = key_sum[...].astype(BF16)
        out[0, :, 2 * width + start : 2 * width + start + step] = value_sum[...].astype(BF16)


def attend_back(qkv, grads, logsum, latent, width):
    _, tokens, _ = qkv.shape
    step = min(128, width)
    spec = lambda columns, at: pl.BlockSpec((1, tokens, columns), lambda l: (at, 0, 0))
    return pl.pallas_call(
        partial(attend_back_kernel, width),
        grid=(1,),
        in_specs=[spec(3 * width, latent), spec(width, 0), spec(width, 0)],
        out_specs=spec(3 * width, 0),
        out_shape=jax.ShapeDtypeStruct((1, tokens, 3 * width), BF16),
        scratch_shapes=[pltpu.VMEM((tokens, step), F32), pltpu.VMEM((tokens, step), F32)],
        compiler_params=pltpu.CompilerParams(vmem_limit_bytes=VMEM_LIMIT),
        cost_estimate=pl.CostEstimate(
            flops=2 * tokens * tokens * width,
            bytes_accessed=18 * tokens * width,
            transcendentals=0,
        ),
    )(qkv, grads, logsum)


def local(
    grid,
    block_in,
    conditioning,
    cotangent,
    ada_weight,
    ada_bias,
    qkv_weight,
    qv_bias,
    out_weight,
    out_bias,
    up_weight,
    up_bias,
    down_weight,
    down_bias,
):
    grid.locate()
    size, at = grid.size, grid.at
    z_n, y_n, c_n, s_n = grid.shape
    _, rows, width = block_in.shape
    hidden = up_weight.shape[1]
    count = grid.count
    groups = c_n * s_n
    head_cols = width // groups
    short = width // count
    long = hidden // count
    block_cols = s_n * long
    half = hidden // 2
    own_group = at["c"] * s_n + at["s"]
    send = grid.send

    cond_own = conditioning[0].astype(F32)
    cond_act = jax.nn.silu(cond_own).astype(BF16)
    shares = jnp.concatenate([qv_bias, out_bias, up_bias, down_bias, cond_act])
    cols = qkv_weight.reshape(short, 3, groups, head_cols)
    blocks = []
    for c_d, s_d in np.ndindex(c_n, s_n):
        target = (at["c"] + c_d) % c_n * s_n + (at["s"] + s_d) % s_n
        part = lax.dynamic_index_in_dim(cols, target, 2, keepdims=False).reshape(short, 3 * head_cols)
        blocks.append(send(part, c=c_d, s=s_d) if c_d + s_d else part)
    x_own = block_in[0]
    shares = after(jnp.broadcast_to(shares[None], (count,) + shares.shape), *blocks)
    qkv_z = grid.gather(jnp.concatenate([block[None] for block in blocks]), "z")
    all_shares = lax.all_to_all(shares, AXES, 0, 0, tiled=True)
    x_all = grid.gather(x_own, "s")
    all_shares = after(all_shares, x_all)
    cuts = np.cumsum([qv_bias.shape[0], out_bias.shape[0], up_bias.shape[0]])
    bias_cols = shares.shape[1] - width
    b_qv, b_out, b_up, b_down = [
        part.reshape(-1).astype(F32) for part in jnp.split(all_shares[:, :bias_cols], cuts, axis=1)
    ]

    cond_all = all_shares[:, bias_cols:].reshape(count // s_n, s_n, width)[:, 0]
    cond_flat = lax.dynamic_slice_in_dim(cond_all, grid.me * short, short, axis=1)
    bias_row = lax.dynamic_update_slice(
        jnp.zeros((6 * width,), F32), ada_bias.astype(F32), (grid.me * ada_bias.shape[0],)
    )
    terms = (dot(cond_flat, ada_weight, (1, 0)) + bias_row).reshape(count, 6 * width // s_n)
    terms = lax.all_to_all(after(terms, qkv_z), AXES, 0, 0, tiled=True)
    small_z = terms
    parts = grid.arrivals(after(qkv_z, terms), "y")
    terms = grid.gather(jnp.sum(terms, axis=0), "s")
    modulation = jnp.concatenate(
        [lax.dynamic_index_in_dim(terms, (at["s"] - s) % s_n, 0, keepdims=False) for s in range(s_n)]
    )
    shift_attn, scale_attn, gate_attn, shift_mlp, scale_mlp, gate_mlp = jnp.split(modulation, 6)

    jobs, table = [], []
    for i, back in enumerate(grid.steps("y", "z")):
        piece, block = divmod(i, z_n)
        for group, (c_d, s_d) in enumerate(np.ndindex(c_n, s_n)):
            jobs.append((piece, block * groups + group, 0, 0))
            table.append(grid.shard_of({**back, "c": c_d, "s": s_d}))
    w_qkv = place([part.reshape(-1, 1, short, 3 * head_cols) for part in parts], jobs, table)

    wide = half // width
    up_cols = up_weight.reshape(short, z_n * y_n, c_n, block_cols)
    up_own = lax.dynamic_index_in_dim(up_cols, at["c"], 2, keepdims=False).reshape(short, wide, width)
    up_other = lax.dynamic_index_in_dim(up_cols, 1 - at["c"], 2, keepdims=False).reshape(short, wide, width)
    up_other = send(after(up_other, x_all), c=1)
    units = [out_weight] + [rows_of[:, i] for rows_of in (up_own, up_other) for i in range(wide)]
    units = jnp.concatenate([unit[None] for unit in units])
    orders = (("s", "y"), ("y", "s"))
    units_z = grid.arrivals(after(units, small_z), "z")
    up_first = [
        grid.arrivals(jnp.concatenate([part[None, low:high] for part in units_z]), order[0])
        for low, high, order in ((0, 1 + wide, orders[0]), (1 + wide, 1 + 2 * wide, orders[1]))
    ]
    inputs = x_own.astype(F32)
    normed_all, inverse_all = normalize(x_all.astype(F32))
    modded_all = (normed_all * (1.0 + scale_attn) + shift_attn).astype(BF16).reshape(s_n * rows, width)
    modded_all = jnp.concatenate([modded_all, send(modded_all, c=1)])
    q_bias = lax.dynamic_index_in_dim(b_qv[:width].reshape(groups, head_cols), own_group, 0, keepdims=False)
    v_bias = lax.dynamic_index_in_dim(b_qv[width:].reshape(groups, head_cols), own_group, 0, keepdims=False)
    qkv_bias = jnp.concatenate([q_bias, jnp.zeros_like(q_bias), v_bias])
    qkv = (dot(modded_all, w_qkv, (1, 0)) + qkv_bias).astype(BF16).reshape(c_n, s_n * rows, 3 * head_cols)
    up_first = [jnp.concatenate([after(part, qkv)[None] for part in parts]) for parts in up_first]
    down_z = grid.arrivals(after(down_weight.reshape(2, long // 2, width), *up_first), "z")
    up_last = [grid.arrivals(after(part, *up_first), order[1]) for part, order in zip(up_first, orders)]
    down_first = [
        grid.gather(jnp.concatenate([part[None, i : i + 1] for part in down_z]), order[0])
        for i, order in enumerate(orders)
    ]
    attended_all, logsums = [], []
    for latent in range(c_n):
        qkv = after(qkv, *(attended_all + down_z if latent else up_first))
        part, logsum = attend(qkv, latent, head_cols)
        attended_all.append(part.reshape(s_n, rows, head_cols))
        logsums.append(logsum)
    arrived = []
    for c_d, s_d in np.ndindex(c_n, s_n):
        part = attended_all[c_d][s_d]
        if c_d + s_d:
            part = after(part, *attended_all)
        arrived.append(send(part, c=-c_d, s=-s_d) if c_d + s_d else part)
    up_steps = [grid.steps(order[1], order[0], "z") for order in orders]
    each = count // (c_n * grid.size["y"])
    flat_last = lax.optimization_barrier(tuple(part for parts in up_last for part in parts) + tuple(attended_all))
    parts = [part.reshape((-1,) + part.shape[2:]) for part in flat_last[: -len(attended_all)]]
    jobs, table, out_jobs, out_table = [], [], [], []
    first = 0
    for c_d, (last, steps) in enumerate(zip(up_last, up_steps)):
        per = len(steps) // len(last)
        for i, back in enumerate(steps):
            piece, block = divmod(i, per)
            for part in range(wide):
                jobs.append((first + piece, block, part + 1 - c_d, part))
                table.append(grid.shard_of({**back, "c": c_d}))
        first += len(last)
    out_own = jnp.concatenate([part[:, :1] for part in parts[: len(up_last[0])]])
    for c_d in range(c_n):
        for i, back in enumerate(up_steps[0]):
            out_jobs.append((c_d, i, 0, 0))
            out_table.append(grid.shard_of({**back, "c": c_d}))
    w_out = place([out_own, send(out_own, c=1)], out_jobs, out_table)
    w_up = place(parts, jobs, table)
    stacked = jnp.stack(arrived)
    ordered = []
    for c in range(c_n):
        for s in range(s_n):
            index = (c - at["c"]) % c_n * s_n + (s - at["s"]) % s_n
            ordered.append(lax.dynamic_index_in_dim(stacked, index, 0, keepdims=False))
    attended = jnp.concatenate(ordered, axis=1)
    down_last = [grid.arrivals(after(part, *arrived), order[1]) for part, order in zip(down_first, orders)]
    attn_proj = dot(after(attended, w_up), w_out, (1, 0)) + b_out
    attn_proj = after(attn_proj, *down_first)
    middle = inputs + gate_attn * attn_proj
    normed_mid, inverse_mid = normalize(middle)
    modded_mlp = (normed_mid * (1.0 + scale_mlp) + shift_mlp).astype(BF16)
    mlp_all = jnp.concatenate([modded_mlp, send(modded_mlp, c=1)])
    up_half = lax.dynamic_index_in_dim(b_up.reshape(-1, c_n, block_cols), at["c"], 1, keepdims=False).reshape(half)
    pre_act = dot(mlp_all, w_up, (1, 0)) + up_half
    gelu_tanh = partial(jax.nn.gelu, approximate=True)
    activated = gelu_tanh(pre_act).astype(BF16)
    out_cot = cotangent[0].astype(F32)
    mlp_grad = (gate_mlp * out_cot).astype(BF16)
    mlp_grad_all = jnp.concatenate([mlp_grad, send(mlp_grad, c=1)])
    down_terms = dot(activated, mlp_grad_all, (0, 0), BF16).reshape(z_n, y_n, s_n, long, width)
    flat_last = lax.optimization_barrier((down_terms,) + tuple(part for parts in down_last for part in parts))
    down_terms = flat_last[0]
    down_a = grid.shed(down_terms[..., : long // 2, :], 2, "s")
    down_sent = grid.sent
    down_b = grid.shed(down_terms[..., long // 2 :, :], 1, "y")
    down_sent = down_sent + grid.sent
    parts = [part.reshape((-1,) + part.shape[2:]) for part in flat_last[1:]]
    jobs, table = [], []
    first = 0
    for row_half, (last, order) in enumerate(zip(down_last, orders)):
        steps = grid.steps(order[1], order[0], "z")
        per = len(steps) // len(last)
        for i, back in enumerate(steps):
            shard = grid.shard_of(back)
            piece, block = divmod(i, per)
            jobs.append((first + piece, block, 0, 0))
            table.append((shard // (c_n * s_n) * s_n + shard % s_n) * 2 + row_half)
        first += len(last)
    w_down = place(parts, jobs, table)
    proj_terms = dot(after(activated, *down_sent), w_down, (1, 0))
    mlp_proj = proj_terms[:rows] + send(proj_terms[rows:], c=1) + b_down
    block_out = (middle + gate_mlp * mlp_proj).astype(BF16)

    down_bias_grad = jnp.sum(mlp_grad.astype(F32), axis=0)
    act_grad = dot(after(mlp_grad_all, proj_terms, *down_sent), w_down, (1, 1))
    _, gelu_back = jax.vjp(gelu_tanh, pre_act)
    pre_grad = gelu_back(act_grad)[0].astype(BF16)
    up_bias_grad = jnp.sum(pre_grad.astype(F32), axis=0)
    down_a, down_b = settle(down_a, BF16, pre_grad), settle(down_b, BF16, pre_grad)
    up_terms = dot(after(mlp_all, down_a, down_b), pre_grad, (0, 0), BF16)
    up_terms = up_terms.reshape(z_n, y_n, c_n, s_n, short, half)
    up_a = grid.shed(lax.dynamic_index_in_dim(up_terms, at["c"], 2, keepdims=False), 1, "y")
    up_sent = grid.sent
    up_b = grid.shed(lax.dynamic_index_in_dim(up_terms, 1 - at["c"], 2, keepdims=False), 2, "s")
    up_sent = up_sent + grid.sent
    down_a, down_b = grid.shed(down_a, 1, "y"), grid.shed(down_b, 1, "s")
    mod_terms = dot(after(pre_grad, *up_sent), w_up, (1, 1))
    arrived = send(mod_terms[rows:].astype(BF16), c=1)
    up_a, up_b = settle(up_a, BF16, mod_terms, arrived), settle(up_b, BF16, mod_terms, arrived)
    mlp_mod_grad = after(mod_terms[:rows], up_a, up_b) + arrived.astype(F32)
    middle_part = normalize_back(mlp_mod_grad * (1.0 + scale_mlp), normed_mid, inverse_mid)
    shift_mlp_grad = jnp.sum(mlp_mod_grad, axis=0)
    scale_mlp_grad = jnp.sum(mlp_mod_grad * normed_mid, axis=0)
    middle_grad = out_cot + middle_part
    gate_mlp_grad = jnp.sum(out_cot * mlp_proj, axis=0)
    attn_grad = (gate_attn * middle_grad).astype(BF16)
    down_terms = jnp.concatenate([settle(part, BF16, attn_grad) for part in (down_a, down_b)], axis=1)
    attn_grad = after(attn_grad, down_terms)
    gate_attn_grad = jnp.sum(middle_grad * attn_proj, axis=0)
    out_bias_grad = jnp.sum(attn_grad.astype(F32), axis=0)
    attended_grad = dot(attn_grad, w_out, (1, 1), BF16)
    arrived = []
    for c_d in range(c_n):
        for s_d in range(s_n):
            target = (at["c"] + c_d) % c_n * s_n + (at["s"] + s_d) % s_n
            part = lax.dynamic_slice_in_dim(attended_grad, target * head_cols, head_cols, axis=1)
            arrived.append(send(part, c=c_d, s=s_d) if c_d + s_d else part)
    up_a, up_b = after(up_a, *arrived), after(up_b, *arrived)
    up_a, up_b = grid.shed(up_a, 1, "s"), grid.shed(up_b, 1, "y")
    down_terms = grid.shed(down_terms, 0, "z")
    out_terms = dot(attended, after(attn_grad, attended_grad), (0, 0), BF16)
    out_terms = out_terms.reshape(z_n, y_n, c_n, s_n, short, width)
    out_terms = grid.reduce(out_terms, 2, "c", BF16)
    out_terms = grid.shed(out_terms, 2, "s")
    out_sent = grid.sent
    qkv_grads = []
    for latent in range(c_n):
        grads = jnp.concatenate(arrived[latent * s_n : (latent + 1) * s_n])[None]
        if latent == 0:
            grads = after(grads, *out_sent)
        else:
            down_weight_grad = settle(down_terms, F32, *qkv_grads)
            up_terms = jnp.concatenate([settle(part, BF16, *qkv_grads) for part in (up_a, up_b)], axis=1)
            up_terms = grid.shed(up_terms, 0, "z")
            grads = after(grads, down_weight_grad, *grid.sent)
        qkv_grads.append(attend_back(qkv, grads, logsums[latent], latent, head_cols))
    qkv_grad = jnp.concatenate(qkv_grads).reshape(c_n * s_n * rows, 3 * head_cols)
    up_terms = settle(up_terms, F32, qkv_grad)
    out_terms = grid.shed(settle(out_terms, BF16, qkv_grad), 1, "y")
    qkv_grad = after(qkv_grad, up_terms, *grid.sent)
    mod_terms = dot(qkv_grad, w_qkv, (1, 1)).reshape(c_n, s_n, rows, width)
    mod_sent = mod_terms[1].astype(BF16)
    qkv_terms = dot(modded_all, after(qkv_grad, mod_sent), (0, 0), BF16)
    qkv_terms = qkv_terms.reshape(z_n, y_n, c_n, s_n, short, 3 * head_cols)
    qkv_terms = grid.shed(qkv_terms, 1, "y")
    qkv_sent = grid.sent
    out_terms = grid.shed(settle(out_terms, BF16, *qkv_sent), 0, "z")
    mod_terms = after(mod_terms[0], *qkv_sent)
    mod_sum = mod_terms + send(mod_sent, c=1).astype(F32)
    shift_attn_grad = jnp.sum(mod_sum, axis=(0, 1))
    scale_attn_grad = jnp.sum(mod_sum * normed_all, axis=(0, 1))
    column_sums = jnp.sum(qkv_grad.astype(F32), axis=0)
    arrived = [send(mod_sum[d].astype(BF16), s=-d) for d in range(1, s_n)]

    modulation_grad = jnp.concatenate(
        [shift_attn_grad, scale_attn_grad, gate_attn_grad, shift_mlp_grad, scale_mlp_grad, gate_mlp_grad]
    )
    def spread(value, index, n, axis):
        shape = value.shape[:axis] + (n,) + value.shape[axis:]
        start = tuple(index if i == axis else 0 for i in range(len(shape)))
        return lax.dynamic_update_slice(jnp.zeros(shape, F32), jnp.expand_dims(value, axis), start)

    q_sums = spread(column_sums[:head_cols], own_group, groups, 0).reshape(-1)
    v_sums = spread(column_sums[2 * head_cols :], own_group, groups, 0).reshape(-1)
    up_sums = spread(up_bias_grad.reshape(-1, block_cols), at["c"], c_n, 1).reshape(-1)
    total = jnp.concatenate([modulation_grad, q_sums, v_sums, out_bias_grad, up_sums, down_bias_grad])
    total = grid.sum_over(total, "s")
    out_weight_grad = settle(out_terms, F32, total)
    qkv_terms = lax.optimization_barrier(tuple(qkv_terms) + (after(total, out_weight_grad),))
    qkv_terms, total = qkv_terms[:-1], qkv_terms[-1]
    total = grid.gather(total, "z")
    qkv_terms = settle(qkv_terms, BF16, total)
    total = grid.gather(total, "c", "y")
    qkv_terms = grid.shed(after(qkv_terms, total), 0, "z")
    total = after(total, *grid.sent)
    attn_mod_grad = mod_sum[0]
    for part in arrived:
        part = after(part, total)
        attn_mod_grad = attn_mod_grad + part.astype(F32)
    input_part = normalize_back(attn_mod_grad * (1.0 + scale_attn), normed_all[0], inverse_all[0])
    input_grad = (middle_grad + input_part).astype(BF16)
    z, y, c = ((at[name] - jnp.arange(size[name])) % size[name] for name in ("z", "y", "c"))
    latent = ((z[None, None] * y_n + y[None, :, None]) * c_n + c[:, None, None]).reshape(-1)
    cond_back = jnp.dot(jax.nn.one_hot(latent, count // s_n, dtype=BF16), cond_flat, preferred_element_type=F32)
    mod_grads = total.reshape(-1, total.shape[-1])[:, : 6 * width]
    cond_terms = lax.dot_general(
        mod_grads, ada_weight.astype(F32), (((1,), (1,)), ((), ())), precision=HIGHEST
    )
    total, mod_grads = lax.optimization_barrier((total, mod_grads, cond_terms))[:2]
    bias_sums = jnp.sum(total.reshape(-1, total.shape[-1]), axis=0)

    def own_share(start, kept):
        return lax.dynamic_slice_in_dim(bias_sums[start : start + kept * count], grid.me * kept, kept)

    ada_bias_grad = own_share(0, ada_bias.shape[0])
    start = 6 * width
    bias_grads = []
    for bias in (qv_bias, out_bias, up_bias, down_bias):
        bias_grads.append(own_share(start, bias.shape[0]))
        start += bias.shape[0] * count
    qv_bias_grad, out_bias_grad, up_bias_grad, down_bias_grad = bias_grads
    ada_weight_grad = lax.dot_general(
        cond_back, mod_grads, (((0,), (0,)), ((), ())), precision=HIGHEST
    )
    order = (latent[:, None] == jnp.arange(count // s_n)[None]).astype(F32)
    cond_terms = lax.dot_general(order, cond_terms, (((0,), (0,)), ((), ())), precision=HIGHEST)
    cond_terms = jnp.broadcast_to(cond_terms[:, None], (count // s_n, s_n, short)).reshape(count, short)
    cond_terms = after(cond_terms, part)
    cond_total = lax.all_to_all(cond_terms, AXES, 0, 0, tiled=True).reshape(width)
    cond_total = after(cond_total, input_grad)
    qkv_terms = settle(qkv_terms, F32, cond_total)
    _, silu_back = jax.vjp(jax.nn.silu, cond_own)
    cond_grad = silu_back(cond_total)[0].astype(BF16)[None]

    up_terms = after(up_terms, total)
    up_first = up_terms[:short].reshape(short, -1, 1, block_cols)
    up_second = up_terms[short:].reshape(short, -1, 1, block_cols)
    up_second = send(up_second, c=1)
    even = at["c"] == 0
    up_weight_grad = jnp.concatenate(
        [jnp.where(even, up_first, up_second), jnp.where(even, up_second, up_first)], axis=2
    ).reshape(short, hidden)
    qkv_terms = qkv_terms.reshape(groups, short, 3 * head_cols)
    arrived, table = [], []
    for c_d, s_d in np.ndindex(c_n, s_n):
        target = (at["c"] + c_d) % c_n * s_n + (at["s"] + s_d) % s_n
        part = lax.dynamic_index_in_dim(qkv_terms, target, 0, keepdims=False)
        arrived.append(send(part, c=c_d, s=s_d) if c_d + s_d else part)
        table.append((at["c"] - c_d) % c_n * s_n + (at["s"] - s_d) % s_n)
    qkv_weight_grad = place_columns(arrived, table, head_cols)
    return (
        block_out[None],
        input_grad[None],
        cond_grad,
        ada_weight_grad,
        ada_bias_grad,
        qkv_weight_grad,
        qv_bias_grad,
        out_weight_grad,
        out_bias_grad,
        up_weight_grad,
        up_bias_grad,
        down_weight_grad,
        down_bias_grad,
    )


def solution(mesh):
    tokens = P("batch", "seq", None)
    vector = P("batch", None)
    matrix, line = P(AXES, None), P(AXES)
    in_specs = (tokens, vector, tokens) + (matrix, line) * 5
    out_specs = (tokens, tokens, vector) + (matrix, line) * 5
    return jax.shard_map(
        partial(local, Grid(mesh)), mesh=mesh, in_specs=in_specs, out_specs=out_specs, check_vma=False
    )
```

```python
from functools import partial

import jax
import jax.numpy as jnp
import numpy as np
from jax import lax
from jax.experimental import pallas as pl
from jax.experimental.pallas import tpu as pltpu
from jax.sharding import PartitionSpec as P

HEAD_DIM = 64
SCALE = HEAD_DIM**-0.5
EPSILON = 1e-06
HIGHEST = lax.Precision.HIGHEST
F32, BF16 = jnp.float32, jnp.bfloat16
AXES = ("batch", "seq")
VMEM_LIMIT = 56 * 1024 * 1024
TILE = 256


def dot(left, right, dims, kind=F32):
    out = lax.dot_general(left, right, ((dims[:1], dims[1:]), ((), ())), preferred_element_type=F32)
    return out.astype(kind)


def after(value, *needed):
    return lax.optimization_barrier((value,) + needed)[0]


def settle(parts, kind, *needed):
    if needed:
        parts = lax.optimization_barrier(tuple(parts) + needed)[: len(parts)]
    return sum(part.astype(F32) for part in parts).astype(kind)


def normalize(values):
    average = jnp.mean(values, axis=-1, keepdims=True)
    centered = values - average
    variance = jnp.mean(centered * centered, axis=-1, keepdims=True)
    inverse = lax.rsqrt(variance + EPSILON)
    return centered * inverse, inverse


def normalize_back(grads, normed, inverse):
    average = jnp.mean(grads, axis=-1, keepdims=True)
    along = jnp.mean(grads * normed, axis=-1, keepdims=True)
    return inverse * (grads - average - normed * along)


class Grid:
    def __init__(self, mesh):
        batch, seq = mesh.shape["batch"], mesh.shape["seq"]
        self.size = {"z": batch // 4, "y": 2, "c": 2, "s": seq}
        self.shape = tuple(self.size.values())
        self.count = batch * seq

    def locate(self):
        batch, seq = lax.axis_index("batch"), lax.axis_index("seq")
        self.at = {"z": batch // 4, "y": (batch // 2) % 2, "c": batch % 2, "s": seq}
        self.me = batch * self.size["s"] + seq

    def send(self, value, **steps):
        moves = [steps.get(name, 0) for name in self.size]
        pairs = []
        for place in np.ndindex(*self.shape):
            target = tuple((p + m) % n for p, m, n in zip(place, moves, self.shape))
            pairs.append(
                (int(np.ravel_multi_index(place, self.shape)), int(np.ravel_multi_index(target, self.shape)))
            )
        return lax.ppermute(value, AXES, pairs)

    def steps(self, *names):
        return [dict(zip(names, at)) for at in np.ndindex(*[self.size[name] for name in names])]

    def arrivals(self, value, *names):
        return [self.send(value, **step) if any(step.values()) else value for step in self.steps(*names)]

    def gather(self, value, *names):
        return jnp.concatenate([part[None] for part in self.arrivals(value, *names)])

    def shed(self, terms, axis, name):
        n, me = self.size[name], self.at[name]
        parts = [lax.dynamic_index_in_dim(terms, (me + d) % n, axis, keepdims=False) for d in range(n)]
        self.sent = parts[1:]
        return [self.send(part, **{name: d}) if d else part for d, part in enumerate(parts)]

    def reduce(self, terms, axis, name, kind):
        return settle(self.shed(terms, axis, name), kind)

    def shard_of(self, back):
        index = 0
        for name, n in self.size.items():
            index = index * n + (self.at[name] - back.get(name, 0)) % n
        return index

    def sum_over(self, value, *names):
        return sum(self.arrivals(value, *names))


def place_kernel(jobs, flat, table, *refs):
    pieces, out, sems = refs[:-2], refs[-2], refs[-1]
    copies = []
    for at, (piece, block, unit, part) in enumerate(jobs):
        source = pieces[piece].at[block, unit]
        rows, columns = source.shape
        if flat:
            target = out.at[
                pl.ds(pl.multiple_of(table[at] * rows, rows), rows), pl.ds(part * columns, columns)
            ]
        else:
            target = out.at[table[at], part]
        copies.append(pltpu.make_async_copy(source, target, sems.at[at]))
        copies[-1].start()
    for copy in copies:
        copy.wait()


def place(pieces, jobs, table):
    rows, columns = pieces[0].shape[2:]
    parts = 1 + max(job[3] for job in jobs)
    count = len(jobs) // parts
    flat = rows % 16 == 0
    out = pl.pallas_call(
        partial(place_kernel, jobs, flat),
        out_shape=jax.ShapeDtypeStruct(
            (count * rows, parts * columns) if flat else (count, parts, rows, columns), pieces[0].dtype
        ),
        grid_spec=pltpu.PrefetchScalarGridSpec(
            num_scalar_prefetch=1,
            in_specs=[pl.BlockSpec(memory_space=pl.ANY)] * len(pieces),
            out_specs=pl.BlockSpec(memory_space=pltpu.VMEM if flat else pl.ANY),
            scratch_shapes=[pltpu.SemaphoreType.DMA((len(jobs),))],
        ),
        compiler_params=pltpu.CompilerParams(vmem_limit_bytes=VMEM_LIMIT),
        cost_estimate=pl.CostEstimate(
            flops=0, bytes_accessed=4 * len(jobs) * rows * columns, transcendentals=0
        ),
    )(jnp.stack(table).astype(jnp.int32), *pieces)
    if not flat:
        out = out.transpose(0, 2, 1, 3).reshape(count * rows, parts * columns)
    return out


def columns_kernel(width, table, *refs):
    pieces, out = refs[:-1], refs[-1]
    total = out.shape[1] // 3
    for at, piece in enumerate(pieces):
        for part in range(3):
            start = pl.multiple_of(part * total + table[at] * width, width)
            out[:, pl.ds(start, width)] = piece[:, part * width : (part + 1) * width]


def place_columns(pieces, table, width):
    rows, total = pieces[0].shape[0], len(pieces) * 3 * width
    if width % 128 != 0:
        out = jnp.zeros((rows, 3, total // 3), F32)
        for piece, group in zip(pieces, table):
            out = lax.dynamic_update_slice(out, piece.reshape(rows, 3, width), (0, 0, group * width))
        return out.reshape(rows, total)
    return pl.pallas_call(
        partial(columns_kernel, width),
        out_shape=jax.ShapeDtypeStruct((rows, total), F32),
        grid_spec=pltpu.PrefetchScalarGridSpec(
            num_scalar_prefetch=1,
            in_specs=[pl.BlockSpec(memory_space=pltpu.VMEM)] * len(pieces),
            out_specs=pl.BlockSpec(memory_space=pltpu.VMEM),
        ),
    )(jnp.stack(table).astype(jnp.int32), *pieces)


def head_mask(width, head):
    lanes = lax.broadcasted_iota(jnp.int32, (1, width), 1)
    return (lanes >= head * HEAD_DIM) & (lanes < (head + 1) * HEAD_DIM)


def attend_kernel(width, qkv, out, logsum):
    tokens = qkv.shape[1]
    step = min(128, width)
    tile = min(TILE, tokens)
    for start in range(0, width, step):
        keys = qkv[0, :, width + start : width + start + step]
        values = qkv[0, :, 2 * width + start : 2 * width + start + step]
        for row in range(0, tokens, tile):
            queries = qkv[0, row : row + tile, start : start + step] * jnp.asarray(SCALE, BF16)
            total, sums = None, None
            for head in range(step // HEAD_DIM):
                mask = head_mask(step, head)
                scores = dot(jnp.where(mask, queries, jnp.zeros_like(queries)), keys, (1, 1))
                top = jnp.max(scores, axis=1, keepdims=True)
                powers = jnp.exp(scores - top)
                weight = jnp.sum(powers, axis=1, keepdims=True)
                part = dot(powers.astype(BF16), values, (1, 0)) / weight
                level = jnp.broadcast_to(top + jnp.log(weight), part.shape)
                total = part if total is None else jnp.where(mask, part, total)
                sums = level if sums is None else jnp.where(mask, level, sums)
            out[0, row : row + tile, start : start + step] = total.astype(BF16)
            logsum[0, row : row + tile, start : start + step] = sums


def attend(qkv, latent, width):
    _, tokens, _ = qkv.shape
    spec = lambda columns, at: pl.BlockSpec((1, tokens, columns), lambda l: (at, 0, 0))
    return pl.pallas_call(
        partial(attend_kernel, width),
        grid=(1,),
        in_specs=[spec(3 * width, latent)],
        out_specs=[spec(width, 0), spec(width, 0)],
        out_shape=[
            jax.ShapeDtypeStruct((1, tokens, width), BF16),
            jax.ShapeDtypeStruct((1, tokens, width), F32),
        ],
        compiler_params=pltpu.CompilerParams(vmem_limit_bytes=VMEM_LIMIT),
        cost_estimate=pl.CostEstimate(
            flops=tokens * tokens * width,
            bytes_accessed=12 * tokens * width,
            transcendentals=0,
        ),
    )(qkv)


def attend_back_kernel(width, qkv, grads, logsum, out, key_sum, value_sum):
    tokens = qkv.shape[1]
    step = min(128, width)
    tile = min(TILE, tokens)
    for start in range(0, width, step):
        keys = qkv[0, :, width + start : width + start + step]
        values = qkv[0, :, 2 * width + start : 2 * width + start + step]
        key_sum[...] = jnp.zeros_like(key_sum)
        value_sum[...] = jnp.zeros_like(value_sum)
        for row in range(0, tokens, tile):
            queries = qkv[0, row : row + tile, start : start + step] * jnp.asarray(SCALE, BF16)
            grad = grads[0, row : row + tile, start : start + step]
            query_grad = None
            for head in range(step // HEAD_DIM):
                mask = head_mask(step, head)
                own_queries = jnp.where(mask, queries, jnp.zeros_like(queries))
                own_grad = jnp.where(mask, grad, jnp.zeros_like(grad))
                lane = start + head * HEAD_DIM
                level = logsum[0, row : row + tile, lane : lane + 1]
                probs = jnp.exp(dot(own_queries, keys, (1, 1)) - level)
                prob_grad = dot(own_grad, values, (1, 1))
                inner = jnp.sum(probs * prob_grad, axis=1, keepdims=True)
                score_grad = (probs * (prob_grad - inner)).astype(BF16)
                part = dot(score_grad, keys, (1, 0))
                query_grad = part if query_grad is None else jnp.where(mask, part, query_grad)
                key_sum[...] += dot(score_grad, own_queries, (0, 0))
                value_sum[...] += dot(probs.astype(BF16), own_grad, (0, 0))
            out[0, row : row + tile, start : start + step] = (query_grad * SCALE).astype(BF16)
        out[0, :, width + start : width + start + step] = key_sum[...].astype(BF16)
        out[0, :, 2 * width + start : 2 * width + start + step] = value_sum[...].astype(BF16)


def attend_back(qkv, grads, logsum, latent, width):
    _, tokens, _ = qkv.shape
    step = min(128, width)
    spec = lambda columns, at: pl.BlockSpec((1, tokens, columns), lambda l: (at, 0, 0))
    return pl.pallas_call(
        partial(attend_back_kernel, width),
        grid=(1,),
        in_specs=[spec(3 * width, latent), spec(width, 0), spec(width, 0)],
        out_specs=spec(3 * width, 0),
        out_shape=jax.ShapeDtypeStruct((1, tokens, 3 * width), BF16),
        scratch_shapes=[pltpu.VMEM((tokens, step), F32), pltpu.VMEM((tokens, step), F32)],
        compiler_params=pltpu.CompilerParams(vmem_limit_bytes=VMEM_LIMIT),
        cost_estimate=pl.CostEstimate(
            flops=2 * tokens * tokens * width,
            bytes_accessed=18 * tokens * width,
            transcendentals=0,
        ),
    )(qkv, grads, logsum)


def local(
    grid,
    block_in,
    conditioning,
    cotangent,
    ada_weight,
    ada_bias,
    qkv_weight,
    qv_bias,
    out_weight,
    out_bias,
    up_weight,
    up_bias,
    down_weight,
    down_bias,
):
    grid.locate()
    size, at = grid.size, grid.at
    z_n, y_n, c_n, s_n = grid.shape
    _, rows, width = block_in.shape
    hidden = up_weight.shape[1]
    count = grid.count
    groups = c_n * s_n
    head_cols = width // groups
    short = width // count
    long = hidden // count
    block_cols = s_n * long
    half = hidden // 2
    own_group = at["c"] * s_n + at["s"]
    send = grid.send

    cond_own = conditioning[0].astype(F32)
    cond_act = jax.nn.silu(cond_own).astype(BF16)
    shares = jnp.concatenate([qv_bias, out_bias, up_bias, down_bias, cond_act])
    cols = qkv_weight.reshape(short, 3, groups, head_cols)
    blocks = []
    for c_d, s_d in np.ndindex(c_n, s_n):
        target = (at["c"] + c_d) % c_n * s_n + (at["s"] + s_d) % s_n
        part = lax.dynamic_index_in_dim(cols, target, 2, keepdims=False).reshape(short, 3 * head_cols)
        blocks.append(send(part, c=c_d, s=s_d) if c_d + s_d else part)
    x_own = block_in[0]
    shares = after(jnp.broadcast_to(shares[None], (count,) + shares.shape), *blocks)
    qkv_z = grid.gather(jnp.concatenate([block[None] for block in blocks]), "z")
    all_shares = lax.all_to_all(shares, AXES, 0, 0, tiled=True)
    x_all = grid.gather(x_own, "s")
    all_shares = after(all_shares, x_all)
    cuts = np.cumsum([qv_bias.shape[0], out_bias.shape[0], up_bias.shape[0]])
    bias_cols = shares.shape[1] - width
    b_qv, b_out, b_up, b_down = [
        part.reshape(-1).astype(F32) for part in jnp.split(all_shares[:, :bias_cols], cuts, axis=1)
    ]

    cond_all = all_shares[:, bias_cols:].reshape(count // s_n, s_n, width)[:, 0]
    cond_flat = lax.dynamic_slice_in_dim(cond_all, grid.me * short, short, axis=1)
    bias_row = lax.dynamic_update_slice(
        jnp.zeros((6 * width,), F32), ada_bias.astype(F32), (grid.me * ada_bias.shape[0],)
    )
    terms = (dot(cond_flat, ada_weight, (1, 0)) + bias_row).reshape(count, 6 * width // s_n)
    terms = lax.all_to_all(after(terms, qkv_z), AXES, 0, 0, tiled=True)
    small_z = terms
    parts = grid.arrivals(after(qkv_z, terms), "y")
    terms = grid.gather(jnp.sum(terms, axis=0), "s")
    modulation = jnp.concatenate(
        [lax.dynamic_index_in_dim(terms, (at["s"] - s) % s_n, 0, keepdims=False) for s in range(s_n)]
    )
    shift_attn, scale_attn, gate_attn, shift_mlp, scale_mlp, gate_mlp = jnp.split(modulation, 6)

    jobs, table = [], []
    for i, back in enumerate(grid.steps("y", "z")):
        piece, block = divmod(i, z_n)
        for group, (c_d, s_d) in enumerate(np.ndindex(c_n, s_n)):
            jobs.append((piece, block * groups + group, 0, 0))
            table.append(grid.shard_of({**back, "c": c_d, "s": s_d}))
    w_qkv = place([part.reshape(-1, 1, short, 3 * head_cols) for part in parts], jobs, table)

    wide = half // width
    up_cols = up_weight.reshape(short, z_n * y_n, c_n, block_cols)
    up_own = lax.dynamic_index_in_dim(up_cols, at["c"], 2, keepdims=False).reshape(short, wide, width)
    up_other = lax.dynamic_index_in_dim(up_cols, 1 - at["c"], 2, keepdims=False).reshape(short, wide, width)
    up_other = send(after(up_other, x_all), c=1)
    units = [out_weight] + [rows_of[:, i] for rows_of in (up_own, up_other) for i in range(wide)]
    units = jnp.concatenate([unit[None] for unit in units])
    orders = (("s", "y"), ("y", "s"))
    units_z = grid.arrivals(after(units, small_z), "z")
    up_first = [
        grid.arrivals(jnp.concatenate([part[None, low:high] for part in units_z]), order[0])
        for low, high, order in ((0, 1 + wide, orders[0]), (1 + wide, 1 + 2 * wide, orders[1]))
    ]
    inputs = x_own.astype(F32)
    normed_all, inverse_all = normalize(x_all.astype(F32))
    modded_all = (normed_all * (1.0 + scale_attn) + shift_attn).astype(BF16).reshape(s_n * rows, width)
    modded_all = jnp.concatenate([modded_all, send(modded_all, c=1)])
    q_bias = lax.dynamic_index_in_dim(b_qv[:width].reshape(groups, head_cols), own_group, 0, keepdims=False)
    v_bias = lax.dynamic_index_in_dim(b_qv[width:].reshape(groups, head_cols), own_group, 0, keepdims=False)
    qkv_bias = jnp.concatenate([q_bias, jnp.zeros_like(q_bias), v_bias])
    qkv = (dot(modded_all, w_qkv, (1, 0)) + qkv_bias).astype(BF16).reshape(c_n, s_n * rows, 3 * head_cols)
    up_first = [jnp.concatenate([after(part, qkv)[None] for part in parts]) for parts in up_first]
    down_z = grid.arrivals(after(down_weight.reshape(2, long // 2, width), *up_first), "z")
    up_last = [grid.arrivals(after(part, *up_first), order[1]) for part, order in zip(up_first, orders)]
    down_first = [
        grid.arrivals(jnp.concatenate([part[None, i : i + 1] for part in down_z]), order[0])
        for i, order in enumerate(orders)
    ]
    attended_all, logsums = [], []
    for latent in range(c_n):
        qkv = after(qkv, *(attended_all + down_z if latent else up_first))
        part, logsum = attend(qkv, latent, head_cols)
        attended_all.append(part.reshape(s_n, rows, head_cols))
        logsums.append(logsum)
    arrived = []
    for c_d, s_d in np.ndindex(c_n, s_n):
        part = attended_all[c_d][s_d]
        if c_d + s_d:
            part = after(part, *attended_all)
        arrived.append(send(part, c=-c_d, s=-s_d) if c_d + s_d else part)
    up_steps = [grid.steps(order[1], order[0], "z") for order in orders]
    each = count // (c_n * grid.size["y"])
    flat_last = lax.optimization_barrier(tuple(part for parts in up_last for part in parts) + tuple(attended_all))
    parts = [part.reshape((-1,) + part.shape[2:]) for part in flat_last[: -len(attended_all)]]
    jobs, table, out_jobs, out_table = [], [], [], []
    first = 0
    for c_d, (last, steps) in enumerate(zip(up_last, up_steps)):
        per = len(steps) // len(last)
        for i, back in enumerate(steps):
            piece, block = divmod(i, per)
            for part in range(wide):
                jobs.append((first + piece, block, part + 1 - c_d, part))
                table.append(grid.shard_of({**back, "c": c_d}))
        first += len(last)
    out_own = jnp.concatenate([part[:, :1] for part in parts[: len(up_last[0])]])
    for c_d in range(c_n):
        for i, back in enumerate(up_steps[0]):
            out_jobs.append((c_d, i, 0, 0))
            out_table.append(grid.shard_of({**back, "c": c_d}))
    w_out = place([out_own, send(out_own, c=1)], out_jobs, out_table)
    w_up = place(parts, jobs, table)
    stacked = jnp.stack(arrived)
    ordered = []
    for c in range(c_n):
        for s in range(s_n):
            index = (c - at["c"]) % c_n * s_n + (s - at["s"]) % s_n
            ordered.append(lax.dynamic_index_in_dim(stacked, index, 0, keepdims=False))
    attended = jnp.concatenate(ordered, axis=1)
    down_first = [
        jnp.concatenate([after(part, w_up, w_out)[None] for part in parts]) for parts in down_first
    ]
    down_last = [grid.arrivals(after(part, *arrived), order[1]) for part, order in zip(down_first, orders)]
    attn_proj = dot(after(attended, w_up), w_out, (1, 0)) + b_out
    attn_proj = after(attn_proj, *down_first)
    middle = inputs + gate_attn * attn_proj
    normed_mid, inverse_mid = normalize(middle)
    modded_mlp = (normed_mid * (1.0 + scale_mlp) + shift_mlp).astype(BF16)
    mlp_all = jnp.concatenate([modded_mlp, send(modded_mlp, c=1)])
    up_half = lax.dynamic_index_in_dim(b_up.reshape(-1, c_n, block_cols), at["c"], 1, keepdims=False).reshape(half)
    pre_act = dot(mlp_all, w_up, (1, 0)) + up_half
    gelu_tanh = partial(jax.nn.gelu, approximate=True)
    activated = gelu_tanh(pre_act).astype(BF16)
    out_cot = cotangent[0].astype(F32)
    mlp_grad = (gate_mlp * out_cot).astype(BF16)
    mlp_grad_all = jnp.concatenate([mlp_grad, send(mlp_grad, c=1)])
    down_terms = dot(activated, mlp_grad_all, (0, 0), BF16).reshape(z_n, y_n, s_n, long, width)
    flat_last = lax.optimization_barrier((down_terms,) + tuple(part for parts in down_last for part in parts))
    down_terms = flat_last[0]
    down_a = grid.shed(down_terms[..., : long // 2, :], 2, "s")
    down_sent = grid.sent
    down_b = grid.shed(down_terms[..., long // 2 :, :], 1, "y")
    down_sent = down_sent + grid.sent
    parts = [part.reshape((-1,) + part.shape[2:]) for part in flat_last[1:]]
    jobs, table = [], []
    first = 0
    for row_half, (last, order) in enumerate(zip(down_last, orders)):
        steps = grid.steps(order[1], order[0], "z")
        per = len(steps) // len(last)
        for i, back in enumerate(steps):
            shard = grid.shard_of(back)
            piece, block = divmod(i, per)
            jobs.append((first + piece, block, 0, 0))
            table.append((shard // (c_n * s_n) * s_n + shard % s_n) * 2 + row_half)
        first += len(last)
    w_down = place(parts, jobs, table)
    proj_terms = dot(after(activated, *down_sent), w_down, (1, 0))
    mlp_proj = proj_terms[:rows] + send(proj_terms[rows:], c=1) + b_down
    block_out = (middle + gate_mlp * mlp_proj).astype(BF16)

    down_bias_grad = jnp.sum(mlp_grad.astype(F32), axis=0)
    act_grad = dot(after(mlp_grad_all, proj_terms, *down_sent), w_down, (1, 1))
    _, gelu_back = jax.vjp(gelu_tanh, pre_act)
    pre_grad = gelu_back(act_grad)[0].astype(BF16)
    up_bias_grad = jnp.sum(pre_grad.astype(F32), axis=0)
    down_a, down_b = settle(down_a, BF16, pre_grad), settle(down_b, BF16, pre_grad)
    up_terms = dot(after(mlp_all, down_a, down_b), pre_grad, (0, 0), BF16)
    up_terms = up_terms.reshape(z_n, y_n, c_n, s_n, short, half)
    up_a = grid.shed(lax.dynamic_index_in_dim(up_terms, at["c"], 2, keepdims=False), 1, "y")
    up_sent = grid.sent
    up_b = grid.shed(lax.dynamic_index_in_dim(up_terms, 1 - at["c"], 2, keepdims=False), 2, "s")
    up_sent = up_sent + grid.sent
    down_a, down_b = grid.shed(down_a, 1, "y"), grid.shed(down_b, 1, "s")
    mod_terms = dot(after(pre_grad, *up_sent), w_up, (1, 1))
    arrived = send(mod_terms[rows:].astype(BF16), c=1)
    up_a, up_b = settle(up_a, BF16, mod_terms, arrived), settle(up_b, BF16, mod_terms, arrived)
    mlp_mod_grad = after(mod_terms[:rows], up_a, up_b) + arrived.astype(F32)
    middle_part = normalize_back(mlp_mod_grad * (1.0 + scale_mlp), normed_mid, inverse_mid)
    shift_mlp_grad = jnp.sum(mlp_mod_grad, axis=0)
    scale_mlp_grad = jnp.sum(mlp_mod_grad * normed_mid, axis=0)
    middle_grad = out_cot + middle_part
    gate_mlp_grad = jnp.sum(out_cot * mlp_proj, axis=0)
    attn_grad = (gate_attn * middle_grad).astype(BF16)
    down_terms = jnp.concatenate([settle(part, BF16, attn_grad) for part in (down_a, down_b)], axis=1)
    attn_grad = after(attn_grad, down_terms)
    gate_attn_grad = jnp.sum(middle_grad * attn_proj, axis=0)
    out_bias_grad = jnp.sum(attn_grad.astype(F32), axis=0)
    attended_grad = dot(attn_grad, w_out, (1, 1), BF16)
    arrived = []
    for c_d in range(c_n):
        for s_d in range(s_n):
            target = (at["c"] + c_d) % c_n * s_n + (at["s"] + s_d) % s_n
            part = lax.dynamic_slice_in_dim(attended_grad, target * head_cols, head_cols, axis=1)
            arrived.append(send(part, c=c_d, s=s_d) if c_d + s_d else part)
    up_a, up_b = after(up_a, *arrived), after(up_b, *arrived)
    up_a, up_b = grid.shed(up_a, 1, "s"), grid.shed(up_b, 1, "y")
    down_terms = grid.shed(down_terms, 0, "z")
    out_terms = dot(attended, after(attn_grad, attended_grad), (0, 0), BF16)
    out_terms = out_terms.reshape(z_n, y_n, c_n, s_n, short, width)
    out_terms = grid.reduce(out_terms, 2, "c", BF16)
    out_terms = grid.shed(out_terms, 2, "s")
    out_sent = grid.sent
    qkv_grads = []
    for latent in range(c_n):
        grads = jnp.concatenate(arrived[latent * s_n : (latent + 1) * s_n])[None]
        if latent == 0:
            grads = after(grads, *out_sent)
        else:
            down_weight_grad = settle(down_terms, F32, *qkv_grads)
            up_terms = jnp.concatenate([settle(part, BF16, *qkv_grads) for part in (up_a, up_b)], axis=1)
            up_terms = grid.shed(up_terms, 0, "z")
            grads = after(grads, down_weight_grad, *grid.sent)
        qkv_grads.append(attend_back(qkv, grads, logsums[latent], latent, head_cols))
    qkv_grad = jnp.concatenate(qkv_grads).reshape(c_n * s_n * rows, 3 * head_cols)
    up_terms = settle(up_terms, F32, qkv_grad)
    out_terms = grid.shed(settle(out_terms, BF16, qkv_grad), 1, "y")
    qkv_grad = after(qkv_grad, up_terms, *grid.sent)
    mod_terms = dot(qkv_grad, w_qkv, (1, 1)).reshape(c_n, s_n, rows, width)
    mod_sent = mod_terms[1].astype(BF16)
    qkv_terms = dot(modded_all, after(qkv_grad, mod_sent), (0, 0), BF16)
    qkv_terms = qkv_terms.reshape(z_n, y_n, c_n, s_n, short, 3 * head_cols)
    qkv_terms = grid.shed(qkv_terms, 1, "y")
    qkv_sent = grid.sent
    out_terms = grid.shed(settle(out_terms, BF16, *qkv_sent), 0, "z")
    mod_terms = after(mod_terms[0], *qkv_sent)
    mod_sum = mod_terms + send(mod_sent, c=1).astype(F32)
    shift_attn_grad = jnp.sum(mod_sum, axis=(0, 1))
    scale_attn_grad = jnp.sum(mod_sum * normed_all, axis=(0, 1))
    column_sums = jnp.sum(qkv_grad.astype(F32), axis=0)
    arrived = [send(mod_sum[d].astype(BF16), s=-d) for d in range(1, s_n)]

    modulation_grad = jnp.concatenate(
        [shift_attn_grad, scale_attn_grad, gate_attn_grad, shift_mlp_grad, scale_mlp_grad, gate_mlp_grad]
    )
    def spread(value, index, n, axis):
        shape = value.shape[:axis] + (n,) + value.shape[axis:]
        start = tuple(index if i == axis else 0 for i in range(len(shape)))
        return lax.dynamic_update_slice(jnp.zeros(shape, F32), jnp.expand_dims(value, axis), start)

    q_sums = spread(column_sums[:head_cols], own_group, groups, 0).reshape(-1)
    v_sums = spread(column_sums[2 * head_cols :], own_group, groups, 0).reshape(-1)
    up_sums = spread(up_bias_grad.reshape(-1, block_cols), at["c"], c_n, 1).reshape(-1)
    total = jnp.concatenate([modulation_grad, q_sums, v_sums, out_bias_grad, up_sums, down_bias_grad])
    total = grid.sum_over(total, "s")
    out_weight_grad = settle(out_terms, F32, total)
    qkv_terms = lax.optimization_barrier(tuple(qkv_terms) + (after(total, out_weight_grad),))
    qkv_terms, total = qkv_terms[:-1], qkv_terms[-1]
    total = grid.gather(total, "z")
    qkv_terms = settle(qkv_terms, BF16, total)
    total = grid.gather(total, "c", "y")
    qkv_terms = grid.shed(after(qkv_terms, total), 0, "z")
    total = after(total, *grid.sent)
    attn_mod_grad = mod_sum[0]
    for part in arrived:
        part = after(part, total)
        attn_mod_grad = attn_mod_grad + part.astype(F32)
    input_part = normalize_back(attn_mod_grad * (1.0 + scale_attn), normed_all[0], inverse_all[0])
    input_grad = (middle_grad + input_part).astype(BF16)
    z, y, c = ((at[name] - jnp.arange(size[name])) % size[name] for name in ("z", "y", "c"))
    latent = ((z[None, None] * y_n + y[None, :, None]) * c_n + c[:, None, None]).reshape(-1)
    cond_back = jnp.dot(jax.nn.one_hot(latent, count // s_n, dtype=BF16), cond_flat, preferred_element_type=F32)
    mod_grads = total.reshape(-1, total.shape[-1])[:, : 6 * width]
    cond_terms = lax.dot_general(
        mod_grads, ada_weight.astype(F32), (((1,), (1,)), ((), ())), precision=HIGHEST
    )
    total, mod_grads = lax.optimization_barrier((total, mod_grads, cond_terms))[:2]
    bias_sums = jnp.sum(total.reshape(-1, total.shape[-1]), axis=0)

    def own_share(start, kept):
        return lax.dynamic_slice_in_dim(bias_sums[start : start + kept * count], grid.me * kept, kept)

    ada_bias_grad = own_share(0, ada_bias.shape[0])
    start = 6 * width
    bias_grads = []
    for bias in (qv_bias, out_bias, up_bias, down_bias):
        bias_grads.append(own_share(start, bias.shape[0]))
        start += bias.shape[0] * count
    qv_bias_grad, out_bias_grad, up_bias_grad, down_bias_grad = bias_grads
    ada_weight_grad = lax.dot_general(
        cond_back, mod_grads, (((0,), (0,)), ((), ())), precision=HIGHEST
    )
    order = (latent[:, None] == jnp.arange(count // s_n)[None]).astype(F32)
    cond_terms = lax.dot_general(order, cond_terms, (((0,), (0,)), ((), ())), precision=HIGHEST)
    cond_terms = jnp.broadcast_to(cond_terms[:, None], (count // s_n, s_n, short)).reshape(count, short)
    cond_terms = after(cond_terms, part)
    cond_total = lax.all_to_all(cond_terms, AXES, 0, 0, tiled=True).reshape(width)
    cond_total = after(cond_total, input_grad)
    qkv_terms = settle(qkv_terms, F32, cond_total)
    _, silu_back = jax.vjp(jax.nn.silu, cond_own)
    cond_grad = silu_back(cond_total)[0].astype(BF16)[None]

    up_terms = after(up_terms, total)
    up_first = up_terms[:short].reshape(short, -1, 1, block_cols)
    up_second = up_terms[short:].reshape(short, -1, 1, block_cols)
    up_second = send(up_second, c=1)
    even = at["c"] == 0
    up_weight_grad = jnp.concatenate(
        [jnp.where(even, up_first, up_second), jnp.where(even, up_second, up_first)], axis=2
    ).reshape(short, hidden)
    qkv_terms = qkv_terms.reshape(groups, short, 3 * head_cols)
    arrived, table = [], []
    for c_d, s_d in np.ndindex(c_n, s_n):
        target = (at["c"] + c_d) % c_n * s_n + (at["s"] + s_d) % s_n
        part = lax.dynamic_index_in_dim(qkv_terms, target, 0, keepdims=False)
        arrived.append(send(part, c=c_d, s=s_d) if c_d + s_d else part)
        table.append((at["c"] - c_d) % c_n * s_n + (at["s"] - s_d) % s_n)
    qkv_weight_grad = place_columns(arrived, table, head_cols)
    return (
        block_out[None],
        input_grad[None],
        cond_grad,
        ada_weight_grad,
        ada_bias_grad,
        qkv_weight_grad,
        qv_bias_grad,
        out_weight_grad,
        out_bias_grad,
        up_weight_grad,
        up_bias_grad,
        down_weight_grad,
        down_bias_grad,
    )


def solution(mesh):
    tokens = P("batch", "seq", None)
    vector = P("batch", None)
    matrix, line = P(AXES, None), P(AXES)
    in_specs = (tokens, vector, tokens) + (matrix, line) * 5
    out_specs = (tokens, tokens, vector) + (matrix, line) * 5
    return jax.shard_map(
        partial(local, Grid(mesh)), mesh=mesh, in_specs=in_specs, out_specs=out_specs, check_vma=False
    )
```
